128 devices in a mesh: fsdp: 16 (over x_hi, z, core), tensor: 8 (over x_lo, y).
Axes of the slice: x: 4 (x_hi: 2, x_lo: 2; x = x_hi * 2 + x_lo), y: 4, z: 4, core: 2. Of those that a mesh axis runs over, the one named last changes fastest.
Arguments:
- tokens: bfloat16 [8192, 4096], P('fsdp'), may hold values from -48 to 48
- token_ids: int32 [8192], P('fsdp'), may hold values from 0 to 128000, as said below
- out_grad: bfloat16 [8192, 4096], P('fsdp', 'tensor'), may hold values from -0.5 to 0.5
- w_query: bfloat16 [4096, 4096], P('fsdp', 'tensor'), may hold values from -0.09375 to 0.09375
- w_key: bfloat16 [4096, 1024], P('fsdp', 'tensor'), may hold values from -0.09375 to 0.09375
- w_value: bfloat16 [4096, 1024], P('fsdp', 'tensor'), may hold values from -0.09375 to 0.09375
- dec_states: bfloat16 [128, 2, 4096], P('fsdp'), may hold values from -48 to 48
- cache_lens: int32 [128], P('fsdp'), may hold values from 1 to 2048, as said below
- key_cache: bfloat16 [128, 2048, 1024], P('fsdp', None, 'tensor'), may hold values from -48 to 48
- value_cache: bfloat16 [128, 2048, 1024], P('fsdp', None, 'tensor'), may hold values from -6 to 6
Outputs:
- grad_query: bfloat16 [4096, 4096], P('fsdp', 'tensor')
- grad_key: bfloat16 [4096, 1024], P('fsdp', 'tensor')
- grad_value: bfloat16 [4096, 1024], P('fsdp', 'tensor')
- input_grad: bfloat16 [8192, 4096], P('fsdp', 'tensor')
- dec_out: bfloat16 [128, 2, 4096], P('fsdp', None, 'tensor')
The draws below stay inside these ranges and needn't reach their ends.
Inputs may be any that keep to these rules, and one draw needn't show every extreme that they name: `token_ids`: position 0 of every block of 512 tokens holds the begin-of-document id 128000, which marks the first position of each packed document; other ids lie below it. `cache_lens`: positions at or past a row's length hold stale entries.
All inputs are finite; a program needn't handle non-finite values.
Results may differ from the reference program's by a relative error of at most 0.035.
Values may be sent and summed in bfloat16 or wider, within the bound.
A program may use at most 128 MiB of HBM per device.

```python
import math
import jax
import jax.numpy as jnp
from jax import lax

D = 4096
HQ = 32
KVH = 8
HD = 128
CACHE = 2048
TOK_DEV = 512
TOKENS = 8192
ROWS = 128
N_FSDP = 16


def scaled_normal(key, shape, top):
    base_key, scale_key = jax.random.split(key)
    base = jax.random.truncated_normal(base_key, -4.0, 4.0, shape, jnp.float32)
    scale_shape = shape[:-1] + (1,)
    scale = jnp.exp(jax.random.uniform(scale_key, scale_shape, jnp.float32, 0.0, math.log(top)))
    return base * scale


def draw_tokens(key, part):
    key = jax.random.fold_in(key, 1)
    top = 1.0
    return scaled_normal(key, (TOKENS, D), top).astype(jnp.bfloat16)


def draw_dec_states(key, part):
    key = jax.random.fold_in(key, 2)
    top = 1.0
    return scaled_normal(key, (ROWS, 2, D), top).astype(jnp.bfloat16)


def draw_key_cache(key, part):
    key = jax.random.fold_in(key, 3)
    top = 1.0
    return scaled_normal(key, (ROWS, CACHE, KVH * HD), top).astype(jnp.bfloat16)


def draw_token_ids(key, part):
    key = jax.random.fold_in(key, 4)
    id_key, start_key = jax.random.split(key)
    drawn = jax.random.randint(id_key, (TOKENS,), 0, 128000)
    starts = jax.random.randint(start_key, (TOKENS,), 0, 128) == 0
    first = jnp.arange(TOKENS) % TOK_DEV == 0
    return jnp.where(starts | first, 128000, drawn).astype(jnp.int32)


def draw_cache_lens(key, part):
    key = jax.random.fold_in(key, 5)
    len_key, pick_key = jax.random.split(key)
    lengths = jax.random.randint(len_key, (ROWS,), 1, CACHE + 1)
    chosen = jax.random.randint(pick_key, (), 0, ROWS)
    return jnp.where(jnp.arange(ROWS) == chosen, CACHE, lengths).astype(jnp.int32)


def shard_levels(rng, shape, shards, least, top_value):
    def one(position, shards_of):
        steps = jax.random.uniform(jax.random.fold_in(jax.random.fold_in(rng, 6), position), (shards_of,), jnp.float32, least / len(shards), top_value / len(shards))
        return jnp.repeat(jnp.exp(steps), shape[position] // shards_of).reshape((-1,) + (1,) * (len(shape) - position - 1))

    loudness = one(*shards[0])
    for cut in shards[1:]:
        loudness = loudness * one(*cut)
    return loudness


def scatter_about(rng, dims, scale, reach, shards=(), kind=jnp.bfloat16):
    drawn = scale * jax.random.normal(rng, dims, jnp.float32)
    if shards:
        drawn = drawn * shard_levels(rng, dims, shards, -0.22, 0.18)
    return jnp.clip(drawn, -reach, reach).astype(kind)


def setup_inputs(seed: int = 0) -> dict:
    key_of = jax.random.split(jax.random.key(seed), 11)
    tokens = draw_tokens(jax.random.fold_in(key_of[10], 71), 0)
    token_ids = draw_token_ids(jax.random.fold_in(key_of[10], 71), 0)
    out_grad = scatter_about(key_of[2], (TOKENS, HQ * HD), 0.0625, 0.5, ((0, 16), (1, 8)))
    w_query = scatter_about(key_of[3], (D, HQ * HD), D ** -0.5, 0.09375, ((0, 16), (1, 8)))
    w_key = scatter_about(key_of[4], (D, KVH * HD), D ** -0.5, 0.09375, ((0, 16), (1, 8)))
    w_value = scatter_about(key_of[5], (D, KVH * HD), D ** -0.5, 0.09375, ((0, 16), (1, 8)))
    dec_states = draw_dec_states(jax.random.fold_in(key_of[10], 71), 0)
    cache_lens = draw_cache_lens(jax.random.fold_in(key_of[10], 71), 0)
    key_cache = draw_key_cache(jax.random.fold_in(key_of[10], 71), 0)
    value_cache = scatter_about(key_of[9], (ROWS, CACHE, KVH * HD), 1.0, 6.0, ((0, 16), (2, 8)))
    return dict(tokens=tokens, token_ids=token_ids, out_grad=out_grad, w_query=w_query, w_key=w_key, w_value=w_value, dec_states=dec_states, cache_lens=cache_lens, key_cache=key_cache, value_cache=value_cache)


learn_rate = 0.004
bos_id = 128000

def as_float(array):
    return array.astype(jnp.float32)

def sequence_grads(x_seq, ids_seq, dout_seq, w_query, w_key, w_value):
    width = x_seq.shape[0]
    groups = HQ // KVH
    scale = 1.0 / math.sqrt(HD)
    query = jnp.dot(x_seq, w_query, preferred_element_type=jnp.float32).astype(jnp.bfloat16).reshape(width, KVH, groups, HD)
    keys = jnp.dot(x_seq, w_key, preferred_element_type=jnp.float32).astype(jnp.bfloat16).reshape(width, KVH, HD)
    values = jnp.dot(x_seq, w_value, preferred_element_type=jnp.float32).astype(jnp.bfloat16).reshape(width, KVH, HD)
    segment = jnp.cumsum((ids_seq == bos_id).astype(jnp.int32))
    place = jnp.arange(width)
    allowed = (place[:, None] >= place[None, :]) & (segment[:, None] == segment[None, :])
    scores = jnp.einsum('ihgd,jhd->hgij', as_float(query), as_float(keys)) * scale
    scores = jnp.where(allowed, scores, -jnp.inf)
    top = lax.optimization_barrier(jnp.max(scores, -1, keepdims=True))
    expo = jnp.exp(scores - top)
    probs = expo / lax.optimization_barrier(jnp.sum(expo, -1, keepdims=True))
    probs_b = probs.astype(jnp.bfloat16)
    upstream = dout_seq.reshape(width, KVH, groups, HD)
    dprob = jnp.einsum('ihgd,jhd->hgij', as_float(upstream), as_float(values))
    delta = lax.optimization_barrier(jnp.sum(probs * dprob, -1, keepdims=True))
    dscore = (probs * (dprob - delta) * scale).astype(jnp.bfloat16)
    grad_q = jnp.einsum('hgij,jhd->ihgd', as_float(dscore), as_float(keys)).astype(jnp.bfloat16)
    grad_k = jnp.einsum('hgij,ihgd->jhd', as_float(dscore), as_float(query)).astype(jnp.bfloat16)
    grad_v = jnp.einsum('hgij,ihgd->jhd', as_float(probs_b), as_float(upstream)).astype(jnp.bfloat16)
    return jnp.concatenate([grad_q.reshape(width, HQ * HD), grad_k.reshape(width, KVH * HD), grad_v.reshape(width, KVH * HD)], 1)

def reference(tokens, token_ids, out_grad, w_query, w_key, w_value, dec_states, cache_lens, key_cache, value_cache):
    q_cols = HQ * HD
    kv_cols = KVH * HD
    columns = q_cols + 2 * kv_cols
    x_blocks = tokens.reshape(N_FSDP, TOK_DEV, D)
    id_blocks = token_ids.reshape(N_FSDP, TOK_DEV)
    dout_blocks = out_grad.reshape(N_FSDP, TOK_DEV, q_cols)

    def step(total, block):
        x_seq, ids_seq, dout_seq = block
        acts = sequence_grads(x_seq, ids_seq, dout_seq, w_query, w_key, w_value)
        part = lax.dot_general(x_seq, acts, (((0,), (0,)), ((), ())), preferred_element_type=jnp.float32)
        return (total + part, acts)
    total, acts = lax.scan(step, jnp.zeros((D, columns), jnp.float32), (x_blocks, id_blocks, dout_blocks))
    grads = (total * (1.0 / N_FSDP)).astype(jnp.bfloat16)
    grad_query = grads[:, :q_cols]
    grad_key = grads[:, q_cols:q_cols + kv_cols]
    grad_value = grads[:, q_cols + kv_cols:]
    acts = acts.reshape(TOKENS, columns)
    weights = jnp.concatenate([w_query, w_key, w_value], 1)
    input_sum = lax.dot_general(acts, weights, (((1,), (1,)), ((), ())), preferred_element_type=jnp.float32)
    input_grad = input_sum.astype(jnp.bfloat16)
    fresh_q = (as_float(w_query) - learn_rate * as_float(grad_query)).astype(jnp.bfloat16)
    fresh_k = (as_float(w_key) - learn_rate * as_float(grad_key)).astype(jnp.bfloat16)
    fresh_v = (as_float(w_value) - learn_rate * as_float(grad_value)).astype(jnp.bfloat16)
    groups = HQ // KVH
    scale = 1.0 / math.sqrt(HD)
    flat = dec_states.reshape(ROWS * 2, D)
    dec_q = jnp.dot(flat, fresh_q, preferred_element_type=jnp.float32).astype(jnp.bfloat16).reshape(ROWS, 2, KVH, groups, HD)
    dec_k = jnp.dot(flat, fresh_k, preferred_element_type=jnp.float32).astype(jnp.bfloat16).reshape(ROWS, 2, KVH, HD)
    dec_v = jnp.dot(flat, fresh_v, preferred_element_type=jnp.float32).astype(jnp.bfloat16).reshape(ROWS, 2, KVH, HD)
    cached_k = key_cache.reshape(ROWS, CACHE, KVH, HD)
    cached_v = value_cache.reshape(ROWS, CACHE, KVH, HD)
    older = jnp.einsum('rshgd,rjhd->rshgj', as_float(dec_q), as_float(cached_k)) * scale
    valid = jnp.arange(CACHE)[None, :] < cache_lens[:, None]
    older = jnp.where(valid[:, None, None, None, :], older, -jnp.inf)
    newer = jnp.einsum('rshgd,rthd->rshgt', as_float(dec_q), as_float(dec_k)) * scale
    causal = jnp.arange(2)[:, None] >= jnp.arange(2)[None, :]
    newer = jnp.where(causal[None, :, None, None, :], newer, -jnp.inf)
    top = jnp.maximum(lax.optimization_barrier(jnp.max(older, -1, keepdims=True)), lax.optimization_barrier(jnp.max(newer, -1, keepdims=True)))
    exp_old = jnp.exp(older - top)
    exp_new = jnp.exp(newer - top)
    denom = lax.optimization_barrier(jnp.sum(exp_old, -1, keepdims=True)) + lax.optimization_barrier(jnp.sum(exp_new, -1, keepdims=True))
    prob_old = (exp_old / denom).astype(jnp.bfloat16)
    prob_new = (exp_new / denom).astype(jnp.bfloat16)
    mixed = jnp.einsum('rshgj,rjhd->rshgd', as_float(prob_old), as_float(cached_v)) + jnp.einsum('rshgt,rthd->rshgd', as_float(prob_new), as_float(dec_v))
    dec_out = mixed.reshape(ROWS, 2, HQ * HD).astype(jnp.bfloat16)
    return (grad_query, grad_key, grad_value, input_grad, dec_out)
```

```python
import math

import jax
import jax.numpy as jnp
from jax import lax
from jax.experimental import pallas as pl
from jax.experimental.pallas import tpu as pltpu
from jax.sharding import PartitionSpec as P

MESH = pl.DeviceIdType.MESH
BF = jnp.bfloat16
F32 = jnp.float32

HD = 128
LEARN_RATE = 0.004
BOS_ID = 128000
MASKED = -1e30

TOK = 512
D = 4096
QC = 512
COLS = 768
ROWS = 256
HALF = ROWS // 2
GROUPS = QC // HD
NF = 16
FEAT = 512
DEC = 16
CACHE = 2048
DROWS = 8

G_SIB = 0
G_P, G_M, G_X, G_PF, G_MF, G_P1, G_M1, G_XF = range(8, 16)
R_SIB = 16
R_X1, R_PQ, R_MQ, R_PB, R_MB, R_PF, R_MF, R_PA, R_MA, R_X2 = range(24, 34)
T_BASE = 34
T_PF, T_MF, T_PB, T_MB, T_PA, T_MA = range(6)
T_X = 46
D_IN = 47
D_OUT = 63
N_MSG = 79

L_TOK, L_OG, L_WQ, L_WK, L_WV, L_DEC, L_KC, L_VC, L_OWN, L_GQ, L_GK, L_GV, L_IG, L_DO, L_OWN2 = range(15)
N_LOCAL = 15

NT = (((1,), (1,)), ((), ()))


def f32_dot(a, b):
    return jnp.dot(a, b, preferred_element_type=F32)


def f32_dot_nt(a, b):
    return lax.dot_general(a, b, NT, preferred_element_type=F32)


def kernel(
    ids, lens, tok_h, og_h, wq_h, wk_h, wv_h, dec_h, kc_h, vc_h,
    gq_o, gk_o, gv_o, ig_o, do_o,
    tok, tok_t, w, proj, pb, og, bias, acts, key_t, gk_acc, gv_acc,
    sbs, acc, rx1, rx0, rm, rp, qm, qp, rfm, rfp,
    part, tfm, tfp, tm, tp, tx, ig, gout,
    kc, vc, dec, dec_in, dp, dpr, dout,
    ssem, rsem, lsem,
):
    f = lax.axis_index("fsdp")
    t = lax.axis_index("tensor")
    xh, z, c = f // 8, (f // 2) % 4, f % 2
    xl, y = t // 4, t % 4

    def fid(dx, dz, dc):
        return ((xh + dx) % 2) * 8 + ((z + dz) % 4) * 2 + (c + dc) % 2

    def tid(dx, dy):
        return ((xl + dx) % 2) * 4 + (y + dy) % 4

    sib = (fid(0, 0, 1), t)
    zp, zm, xp = (fid(0, 1, 0), t), (fid(0, 3, 0), t), (fid(1, 0, 0), t)
    yp, ym, xt = (f, tid(0, 1)), (f, tid(0, 3)), (f, tid(1, 0))

    def local(src, dst, i):
        return pltpu.make_async_copy(src, dst, lsem.at[i])

    sent = []

    def msg(i, src, dst, to):
        return pltpu.make_async_remote_copy(
            src_ref=src, dst_ref=dst, send_sem=ssem.at[i], recv_sem=rsem.at[i], device_id=to, device_id_type=MESH
        )

    def send(i, src, dst, to):
        m = msg(i, src, dst, to)
        m.start()
        sent.append(m)

    def arrived(i, ref, to):
        msg(i, ref, ref, to).wait_recv()

    def peer(k):
        return lax.rem(f + k, NF)

    own_w = w.at[f]
    loads = [
        local(wq_h, own_w.at[:, pl.ds(0, QC)], L_WQ),
        local(wk_h, own_w.at[:, pl.ds(QC, HD)], L_WK),
        local(wv_h, own_w.at[:, pl.ds(QC + HD, HD)], L_WV),
    ]
    for m in loads:
        m.start()
    load_dec = local(dec_h, dec, L_DEC)
    load_dec.start()
    load_tok = local(tok_h, tok, L_TOK)
    load_tok.start()
    load_og = local(og_h, og, L_OG)
    load_og.start()

    barrier = pltpu.get_barrier_semaphore()
    for k in range(1, NF):
        pl.semaphore_signal(barrier, inc=1, device_id=(peer(k), t), device_id_type=MESH)
    for to in (yp, ym, xt):
        pl.semaphore_signal(barrier, inc=1, device_id=to, device_id_type=MESH)
    for m in loads:
        m.wait()
    pl.semaphore_wait(barrier, NF + 2)

    send(G_P, own_w, own_w, zp)
    send(G_M, own_w, own_w, zm)
    send(G_X, own_w, own_w, xp)
    send(G_SIB, own_w, own_w, sib)

    load_dec.wait()

    def dec_piece(k):
        to = peer(k)
        return msg(
            D_IN + k,
            dec.at[:, pl.ds(pl.multiple_of(to * ROWS, ROWS), ROWS)],
            dec_in.at[pl.ds(pl.multiple_of(f * DEC, DEC), DEC), :],
            (to, t),
        )

    def send_dec(k, carry):
        dec_piece(k).start()
        return carry

    lax.fori_loop(1, NF, send_dec, 0)
    own_dec = local(
        dec.at[:, pl.ds(pl.multiple_of(f * ROWS, ROWS), ROWS)],
        dec_in.at[pl.ds(pl.multiple_of(f * DEC, DEC), DEC), :],
        L_OWN,
    )
    own_dec.start()
    load_kc = local(kc_h, kc, L_KC)
    load_vc = local(vc_h, vc, L_VC)
    load_kc.start()
    load_vc.start()

    bos = (ids[...] == BOS_ID).astype(F32)
    row = lax.broadcasted_iota(jnp.int32, (TOK, TOK), 0)
    col = lax.broadcasted_iota(jnp.int32, (TOK, TOK), 1)
    seg_row = f32_dot(jnp.broadcast_to(bos, (16, TOK)).astype(BF), (row <= col).astype(BF))
    seg_col = f32_dot_nt((col <= row).astype(BF), jnp.broadcast_to(bos, (HD, TOK)).astype(BF))
    seg_col = jnp.concatenate([seg_col] * (TOK // HD), axis=1)
    bias[...] = jnp.where((row <= col) & (seg_col == seg_row[0:1, :]), 0.0, MASKED)

    load_tok.wait()

    def turn(i, carry):
        at = pl.ds(pl.multiple_of(i * ROWS, ROWS), ROWS)
        tok_t[at, :] = tok[:, at].T
        return carry

    lax.fori_loop(0, NF, turn, 0)

    def project(dx, dz, first=False):
        chip = fid(dx, dz, 0) // 2
        at = pl.ds(pl.multiple_of(chip * 2 * ROWS, 2 * ROWS), 2 * ROWS)
        rows = w[pl.ds(chip * 2, 2)].reshape(2 * ROWS, COLS)
        term = f32_dot(tok[:, at], rows)
        proj[...] = term if first else proj[...] + term

    def shard(dx, dz, dc=0):
        return w.at[fid(dx, dz, dc)]

    def pass_on(dx, dz):
        send(G_SIB + dx * 4 + dz, shard(dx, dz), shard(dx, dz), sib)

    def from_sib(dx, dz):
        arrived(G_SIB + dx * 4 + dz, shard(dx, dz, 1), sib)

    from_sib(0, 0)
    project(0, 0, True)

    top, bottom = pl.ds(0, HALF), pl.ds(HALF, HALF)
    arrived(G_P, shard(0, 3), zp)
    send(G_PF, shard(0, 3).at[top], shard(0, 3).at[top], zp)
    arrived(G_M, shard(0, 1), zm)
    send(G_MF, shard(0, 1).at[bottom], shard(0, 1).at[bottom], zm)
    arrived(G_X, shard(1, 0), xp)
    send(G_P1, shard(1, 0), shard(1, 0), zp)
    send(G_M1, shard(1, 0), shard(1, 0), zm)
    pass_on(0, 3)
    pass_on(0, 1)
    pass_on(1, 0)
    for at in ((0, 3), (0, 1), (1, 0)):
        from_sib(*at)
        project(*at)
    arrived(G_PF, shard(0, 2).at[top], zp)
    arrived(G_MF, shard(0, 2).at[bottom], zm)
    send(G_XF, shard(0, 2), shard(0, 2), xp)
    pass_on(0, 2)
    from_sib(0, 2)
    project(0, 2)
    arrived(G_P1, shard(1, 3), zp)
    pass_on(1, 3)
    arrived(G_M1, shard(1, 1), zm)
    pass_on(1, 1)
    from_sib(1, 3)
    project(1, 3)
    from_sib(1, 1)
    project(1, 1)
    arrived(G_XF, shard(1, 2), xp)
    pass_on(1, 2)
    from_sib(1, 2)
    project(1, 2)

    pb[...] = proj[...].astype(BF)
    load_og.wait()
    key_t[...] = pb[:, QC:QC + HD].T
    gk_acc[...] = jnp.zeros_like(gk_acc)
    gv_acc[...] = jnp.zeros_like(gv_acc)
    scale = 1.0 / math.sqrt(HD)
    width = TOK // 2

    def head(h, carry):
        at = pl.ds(pl.multiple_of(h * HD, HD), HD)
        for block in range(2):
            qs = pl.ds(block * width, width)
            seen = (block + 1) * width
            ks = pl.ds(0, seen)
            keys = pb[ks, pl.ds(QC, HD)]
            values = pb[ks, pl.ds(QC + HD, HD)]
            query = pb[qs, at]
            upstream = og[qs, at]
            scores = f32_dot_nt(keys, query) * scale + bias[ks, qs]
            expo = jnp.exp(scores - jnp.max(scores, 0, keepdims=True))
            probs = expo * (1.0 / jnp.sum(expo, 0, keepdims=True))
            dprob = f32_dot_nt(values, upstream)
            delta = jnp.sum(probs * dprob, 0, keepdims=True)
            dscore = (probs * (dprob - delta) * scale).astype(BF)
            gv_acc[ks, :] += f32_dot(probs.astype(BF), upstream)
            gk_acc[ks, :] += f32_dot(dscore, query)
            acts[qs, at] = f32_dot(key_t[:, ks], dscore).T.astype(BF)
        return carry

    lax.fori_loop(0, GROUPS, head, 0)
    acts[:, QC:QC + HD] = gk_acc[...].astype(BF)
    acts[:, QC + HD:] = gv_acc[...].astype(BF)

    def grad_block(slot):
        rows = tok_t[pl.ds(pl.multiple_of(slot * ROWS, ROWS), ROWS), :]
        return f32_dot(rows, acts[...])

    def chip_of(i):
        return i // 4, i % 4

    def to_sib(i):
        return msg(R_SIB + i, sbs.at[i], acc.at[i], sib)

    def sib_block(k, carry):
        i = 7 - k
        dx, dz = chip_of(i)
        sbs[i] = grad_block(fid(dx, dz, 1)).astype(BF)
        to_sib(i).start()
        return carry

    def own_block(i, carry):
        dx, dz = chip_of(i)
        block = grad_block(fid(dx, dz, 0))
        arrived(R_SIB + i, acc.at[i], sib)
        acc[i] = (block + acc[i].astype(F32)).astype(BF)
        return carry

    def add(dst, *terms):
        total = dst[...].astype(F32)
        for x in terms:
            total = total + x[...].astype(F32)
        dst[...] = total.astype(BF)

    lax.fori_loop(0, 8, sib_block, 0)
    lax.fori_loop(4, 8, own_block, 0)
    send(R_X1, acc.at[6], rx1, xp)
    send(R_PQ, acc.at[5], qm, zp)
    send(R_MQ, acc.at[7], qp, zm)
    lax.fori_loop(0, 4, own_block, 0)
    send(R_PB, acc.at[1, bottom], rm.at[bottom], zp)
    send(R_MB, acc.at[3, top], rp.at[top], zm)

    t_top, t_bottom = pl.ds(0, TOK // 2), pl.ds(TOK // 2, TOK // 2)

    def input_block(i, carry):
        dx, dy = chip_of(i)
        rows = w[pl.ds(tid(dx, dy) * 2, 2)].reshape(2 * ROWS, COLS)
        part[i] = f32_dot_nt(acts[...], rows).astype(BF)
        return carry

    def send_near(dx):
        base, i = T_BASE + dx * 6, dx * 4
        send(base + T_PF, part.at[i + 2, t_top], tfp.at[dx], yp)
        send(base + T_MF, part.at[i + 2, t_bottom], tfm.at[dx], ym)
        send(base + T_PB, part.at[i + 1, t_bottom], tm.at[dx, t_bottom], yp)
        send(base + T_MB, part.at[i + 3, t_top], tp.at[dx, t_top], ym)

    def send_relayed(dx):
        base, i = T_BASE + dx * 6, dx * 4
        arrived(base + T_PF, tfp.at[dx], yp)
        add(part.at[i + 1, t_top], tfp.at[dx])
        send(base + T_PA, part.at[i + 1, t_top], tm.at[dx, t_top], yp)
        arrived(base + T_MF, tfm.at[dx], ym)
        add(part.at[i + 3, t_bottom], tfm.at[dx])
        send(base + T_MA, part.at[i + 3, t_bottom], tp.at[dx, t_bottom], ym)

    def ring_arrived(dx):
        base = T_BASE + dx * 6
        arrived(base + T_PB, tm.at[dx, t_bottom], yp)
        arrived(base + T_MB, tp.at[dx, t_top], ym)
        arrived(base + T_PA, tm.at[dx, t_top], yp)
        arrived(base + T_MA, tp.at[dx, t_bottom], ym)

    lax.fori_loop(4, 8, input_block, 0)
    send_near(1)
    lax.fori_loop(0, 4, input_block, 0)

    arrived(R_X1, rx1, xp)
    add(acc.at[2], rx1)
    send(R_PF, acc.at[2, top], rfp, zp)
    send(R_MF, acc.at[2, bottom], rfm, zm)
    arrived(R_PQ, qm, zp)
    arrived(R_MQ, qp, zm)
    add(acc.at[4], qm, qp)
    send(R_X2, acc.at[4], rx0, xp)
    send_relayed(1)
    send_near(0)
    arrived(R_PF, rfp, zp)
    add(acc.at[1, top], rfp)
    send(R_PA, acc.at[1, top], rm.at[top], zp)
    arrived(R_MF, rfm, zm)
    add(acc.at[3, bottom], rfm)
    send(R_MA, acc.at[3, bottom], rp.at[bottom], zm)
    ring_arrived(1)
    add(part.at[4], tm.at[1], tp.at[1])
    send(T_X, part.at[4], tx, xt)
    send_relayed(0)

    arrived(R_PB, rm.at[bottom], zp)
    arrived(R_MB, rp.at[top], zm)
    arrived(R_PA, rm.at[top], zp)
    arrived(R_MA, rp.at[bottom], zm)
    arrived(R_X2, rx0, xp)
    total = acc[0].astype(F32) + rm[...].astype(F32) + rp[...].astype(F32) + rx0[...].astype(F32)
    grad = (total * (1.0 / NF)).astype(BF)
    gout[...] = grad
    stores = [
        local(gout.at[:, pl.ds(0, QC)], gq_o, L_GQ),
        local(gout.at[:, pl.ds(QC, HD)], gk_o, L_GK),
        local(gout.at[:, pl.ds(QC + HD, HD)], gv_o, L_GV),
    ]
    for m in stores:
        m.start()
    fresh = (own_w[...].astype(F32) - LEARN_RATE * grad.astype(F32)).astype(BF)

    def dec_arrived(k, carry):
        at = pl.ds(pl.multiple_of(peer(NF - k) * DEC, DEC), DEC)
        arrived(D_IN + k, dec_in.at[at, :], (peer(k), t))
        return carry

    lax.fori_loop(1, NF, dec_arrived, 0)
    own_dec.wait()
    dp[...] = f32_dot(dec_in[...], fresh).astype(BF)

    def dec_out_piece(k):
        to = peer(k)
        return msg(
            D_OUT + k,
            dp.at[pl.ds(pl.multiple_of(to * DEC, DEC), DEC), :],
            dpr.at[pl.ds(pl.multiple_of(f * DEC, DEC), DEC), :],
            (to, t),
        )

    def send_dec_out(k, carry):
        dec_out_piece(k).start()
        return carry

    lax.fori_loop(1, NF, send_dec_out, 0)
    own_rows = pl.ds(pl.multiple_of(f * DEC, DEC), DEC)
    own_part = local(dp.at[own_rows, :], dpr.at[own_rows, :], L_OWN2)
    own_part.start()
    load_kc.wait()
    load_vc.wait()

    def dec_out_arrived(k, carry):
        at = pl.ds(pl.multiple_of(peer(NF - k) * DEC, DEC), DEC)
        arrived(D_OUT + k, dpr.at[at, :], (peer(k), t))
        return carry

    lax.fori_loop(1, NF, dec_out_arrived, 0)
    own_part.wait()
    dsum = dpr[0:DEC, :].astype(F32)
    for k in range(1, NF):
        dsum = dsum + dpr[k * DEC:(k + 1) * DEC, :].astype(F32)
    dsum = dsum.astype(BF)

    dec_q = dsum[:, :QC].astype(F32)
    dec_k = dsum[:, QC:QC + HD]
    dec_v = dsum[:, QC + HD:]
    n_q = 2 * GROUPS
    place = lax.broadcasted_iota(jnp.int32, (n_q, CACHE), 1)
    new_col = lax.broadcasted_iota(jnp.int32, (n_q, DEC), 1)
    new_step = lax.broadcasted_iota(jnp.int32, (n_q, DEC), 0) % 2
    for r in range(DROWS):
        q = jnp.concatenate([dec_q[2 * r:2 * r + 2, g * HD:(g + 1) * HD] for g in range(GROUPS)], axis=0).astype(BF)
        older = jnp.where(place < lens[r], f32_dot_nt(q, kc[r]) * scale, MASKED)
        visible = (new_col // 2 == r) & (new_col % 2 <= new_step)
        newer = jnp.where(visible, f32_dot_nt(q, dec_k) * scale, MASKED)
        best = jnp.maximum(jnp.max(older, 1, keepdims=True), jnp.max(newer, 1, keepdims=True))
        exp_old = jnp.exp(older - best)
        exp_new = jnp.exp(newer - best)
        inv = 1.0 / (jnp.sum(exp_old, 1, keepdims=True) + jnp.sum(exp_new, 1, keepdims=True))
        mixed = f32_dot((exp_old * inv).astype(BF), vc[r]) + f32_dot((exp_new * inv).astype(BF), dec_v)
        for g in range(GROUPS):
            dout[2 * r:2 * r + 2, g * HD:(g + 1) * HD] = mixed[2 * g:2 * g + 2, :]
    do_o[...] = dout[...].astype(BF)

    ring_arrived(0)
    arrived(T_X, tx, xt)
    total = part[0].astype(F32) + tm[0].astype(F32) + tp[0].astype(F32) + tx[...].astype(F32)
    ig[...] = total.astype(BF)
    store_ig = local(ig, ig_o, L_IG)
    store_ig.start()
    stores.append(store_ig)

    for m in sent:
        m.wait_send()

    def sent_small(k, carry):
        dec_piece(k).wait_send()
        dec_out_piece(k).wait_send()
        return carry

    lax.fori_loop(1, NF, sent_small, 0)

    def sent_sib(i, carry):
        to_sib(i).wait_send()
        return carry

    lax.fori_loop(0, 8, sent_sib, 0)
    for m in stores:
        m.wait()


def on_device(tokens, token_ids, out_grad, w_query, w_key, w_value, dec_states, cache_lens, key_cache, value_cache):
    anywhere = pl.BlockSpec(memory_space=pl.ANY)
    vmem = pl.BlockSpec(memory_space=pltpu.VMEM)

    def buf(*shape, dtype=BF):
        return pltpu.VMEM(shape, dtype)

    shapes = [(ROWS, QC), (ROWS, HD), (ROWS, HD), (TOK, FEAT), (DEC, QC)]
    *grads, dec_out = pl.pallas_call(
        kernel,
        out_shape=[jax.ShapeDtypeStruct(s, BF) for s in shapes],
        in_specs=[vmem, pl.BlockSpec(memory_space=pltpu.SMEM)] + [anywhere] * 8,
        out_specs=[anywhere] * 4 + [vmem],
        scratch_shapes=[
            buf(TOK, D), buf(D, TOK), buf(NF, ROWS, COLS), buf(TOK, COLS, dtype=F32), buf(TOK, COLS), buf(TOK, QC),
            buf(TOK, TOK, dtype=F32), buf(TOK, COLS), buf(HD, TOK), buf(TOK, HD, dtype=F32), buf(TOK, HD, dtype=F32),
            buf(8, ROWS, COLS), buf(8, ROWS, COLS),
            buf(ROWS, COLS), buf(ROWS, COLS), buf(ROWS, COLS), buf(ROWS, COLS), buf(ROWS, COLS), buf(ROWS, COLS),
            buf(HALF, COLS), buf(HALF, COLS),
            buf(8, TOK, FEAT), buf(2, TOK // 2, FEAT), buf(2, TOK // 2, FEAT), buf(2, TOK, FEAT), buf(2, TOK, FEAT),
            buf(TOK, FEAT), buf(TOK, FEAT), buf(ROWS, COLS),
            buf(DROWS, CACHE, HD), buf(DROWS, CACHE, HD),
            buf(DEC, D), buf(NF * DEC, ROWS), buf(NF * DEC, COLS), buf(NF * DEC, COLS), buf(DEC, QC, dtype=F32),
            pltpu.SemaphoreType.DMA((N_MSG,)), pltpu.SemaphoreType.DMA((N_MSG,)), pltpu.SemaphoreType.DMA((N_LOCAL,)),
        ],
        compiler_params=pltpu.CompilerParams(collective_id=0, has_side_effects=True, vmem_limit_bytes=60 << 20),
        cost_estimate=pl.CostEstimate(flops=13 * 10**9, bytes_accessed=16 * 10**6, transcendentals=2 * 10**6),
    )(
        token_ids.reshape(1, TOK), cache_lens, tokens, out_grad, w_query, w_key, w_value,
        dec_states.reshape(DEC, D), key_cache, value_cache,
    )
    return (*grads, dec_out.reshape(DROWS, 2, QC))


def solution(mesh):
    placed = (
        P("fsdp", None),
        P("fsdp"),
        P("fsdp", "tensor"),
        P("fsdp", "tensor"),
        P("fsdp", "tensor"),
        P("fsdp", "tensor"),
        P("fsdp", None, None),
        P("fsdp"),
        P("fsdp", None, "tensor"),
        P("fsdp", None, "tensor"),
    )
    return jax.shard_map(
        on_device,
        mesh=mesh,
        in_specs=placed,
        out_specs=(
            P("fsdp", "tensor"),
            P("fsdp", "tensor"),
            P("fsdp", "tensor"),
            P("fsdp", "tensor"),
            P("fsdp", None, "tensor"),
        ),
        check_vma=False,
    )
```

```python
import math

import jax
import jax.numpy as jnp
from jax import lax
from jax.experimental import pallas as pl
from jax.experimental.pallas import tpu as pltpu
from jax.sharding import PartitionSpec as P

MESH = pl.DeviceIdType.MESH
BF = jnp.bfloat16
F32 = jnp.float32

HD = 128
LEARN_RATE = 0.004
BOS_ID = 128000
MASKED = -1e30

TOK = 512
D = 4096
QC = 512
COLS = 768
ROWS = 256
HALF = ROWS // 2
GROUPS = QC // HD
NF = 16
FEAT = 512
DEC = 16
CACHE = 2048
DROWS = 8

G_SIB = 0
G_PT, G_PB, G_MT, G_MB, G_X, G_PF, G_MF, G_XA, G_XB, G_P1, G_M1, G_P2, G_M2 = range(8, 21)
R_SIB = 21
R_X1T, R_X1B, R_PQ, R_MQ, R_PB, R_MB, R_PF, R_MF, R_PA, R_MA, R_X2 = range(29, 40)
T_BASE = 40
T_PF, T_MF, T_PB, T_MB, T_PA, T_MA = range(6)
T_X = 52
D_IN = 53
D_OUT = 69
N_MSG = 85

L_TOK, L_OG, L_WQ, L_WK, L_WV, L_DEC, L_KC, L_VC, L_OWN, L_GQ, L_GK, L_GV, L_IG, L_DO, L_OWN2 = range(15)
N_LOCAL = 15

NT = (((1,), (1,)), ((), ()))


def f32_dot(a, b):
    return jnp.dot(a, b, preferred_element_type=F32)


def f32_dot_nt(a, b):
    return lax.dot_general(a, b, NT, preferred_element_type=F32)


def kernel(
    ids, lens, tok_h, og_h, wq_h, wk_h, wv_h, dec_h, kc_h, vc_h,
    gq_o, gk_o, gv_o, ig_o, do_o,
    tok, tok_t, w, proj, pb, og, bias, acts, key_t, gk_acc, gv_acc,
    sbs, acc, rx1, rx0, rm, rp, qm, qp, rfm, rfp,
    part, tfm, tfp, tm, tp, tx, ig, gout,
    kc, vc, dec3, dec_f32, dec, dec_in, dp, dpr,
    ssem, rsem, lsem,
):
    f = lax.axis_index("fsdp")
    t = lax.axis_index("tensor")
    xh, z, c = f // 8, (f // 2) % 4, f % 2
    xl, y = t // 4, t % 4

    sense = 1 + 2 * c

    def fid(dx, dz, dc):
        return ((xh + dx) % 2) * 8 + ((z + sense * dz) % 4) * 2 + (c + dc) % 2

    def place_of(dx, dz):
        return dx * 4 + (sense * dz) % 4

    def tid(dx, dy):
        return ((xl + dx) % 2) * 4 + (y + dy) % 4

    sib = (fid(0, 0, 1), t)
    zp, zm, xp = (fid(0, 1, 0), t), (fid(0, 3, 0), t), (fid(1, 0, 0), t)
    yp, ym, xt = (f, tid(0, 1)), (f, tid(0, 3)), (f, tid(1, 0))

    def local(src, dst, i):
        return pltpu.make_async_copy(src, dst, lsem.at[i])

    sent = []

    def msg(i, src, dst, to):
        return pltpu.make_async_remote_copy(
            src_ref=src, dst_ref=dst, send_sem=ssem.at[i], recv_sem=rsem.at[i], device_id=to, device_id_type=MESH
        )

    def send(i, src, dst, to):
        m = msg(i, src, dst, to)
        m.start()
        sent.append(m)

    def arrived(i, ref, to):
        msg(i, ref, ref, to).wait_recv()

    def peer(k):
        return lax.rem(f + k, NF)

    near = (sib, zp, zm, xp, yp, ym, xt)
    barrier = pltpu.get_barrier_semaphore()
    for to in near:
        pl.semaphore_signal(barrier, inc=1, device_id=to, device_id_type=MESH)
    own_w = w.at[f]
    loads = [
        local(wq_h, own_w.at[:, pl.ds(0, QC)], L_WQ),
        local(wk_h, own_w.at[:, pl.ds(QC, HD)], L_WK),
        local(wv_h, own_w.at[:, pl.ds(QC + HD, HD)], L_WV),
    ]
    for m in loads:
        m.start()
    load_tok = local(tok_h, tok, L_TOK)
    load_tok.start()
    load_dec = local(dec_h, dec3, L_DEC)
    load_dec.start()
    load_og = local(og_h, og, L_OG)
    load_og.start()

    for m in loads:
        m.wait()
    pl.semaphore_wait(barrier, len(near))

    top, bottom = pl.ds(0, HALF), pl.ds(HALF, HALF)
    send(G_PT, own_w.at[top], own_w.at[top], zp)
    send(G_MB, own_w.at[bottom], own_w.at[bottom], zm)
    send(G_X, own_w, own_w, xp)
    send(G_PB, own_w.at[bottom], own_w.at[bottom], zp)
    send(G_MT, own_w.at[top], own_w.at[top], zm)
    send(G_SIB + place_of(0, 0), own_w, own_w, sib)

    load_kc = local(kc_h, kc, L_KC)
    load_vc = local(vc_h, vc, L_VC)
    load_kc.start()
    load_vc.start()

    bos = (ids[...] == BOS_ID).astype(F32)
    row = lax.broadcasted_iota(jnp.int32, (TOK, TOK), 0)
    col = lax.broadcasted_iota(jnp.int32, (TOK, TOK), 1)
    seg_row = f32_dot(jnp.broadcast_to(bos, (16, TOK)).astype(BF), (row <= col).astype(BF))
    seg_col = f32_dot_nt((col <= row).astype(BF), jnp.broadcast_to(bos, (HD, TOK)).astype(BF))
    seg_col = jnp.concatenate([seg_col] * (TOK // HD), axis=1)
    bias[...] = jnp.where((row <= col) & (seg_col == seg_row[0:1, :]), 0.0, MASKED)

    load_dec.wait()
    for r in range(DROWS):
        dec_f32[2 * r:2 * r + 2, :] = dec3[r].astype(F32)
    dec[...] = dec_f32[...].astype(BF)
    load_tok.wait()

    def turn(i, carry):
        at = pl.ds(pl.multiple_of(i * ROWS, ROWS), ROWS)
        tok_t[at, :] = tok[:, at].T
        return carry

    def project(dx, dz, first=False):
        chip = fid(dx, dz, 0) // 2
        at = pl.ds(pl.multiple_of(chip * 2 * ROWS, 2 * ROWS), 2 * ROWS)
        rows = w[pl.ds(chip * 2, 2)].reshape(2 * ROWS, COLS)
        term = f32_dot(tok[:, at], rows)
        proj[...] = term if first else proj[...] + term

    def shard(dx, dz, dc=0):
        return w.at[fid(dx, dz, dc)]

    def pass_on(dx, dz):
        send(G_SIB + place_of(dx, dz), shard(dx, dz), shard(dx, dz), sib)

    def from_sib(dx, dz):
        arrived(G_SIB + place_of(dx, dz), shard(dx, dz, 1), sib)

    def relay(i, ref, to):
        send(i, ref, ref, to)

    from_sib(0, 0)
    project(0, 0, True)
    lax.fori_loop(0, 4, turn, 0)

    arrived(G_PT, shard(0, 3).at[top], zp)
    relay(G_PF, shard(0, 3).at[top], zp)
    relay(G_XA, shard(0, 3).at[top], xp)
    arrived(G_MB, shard(0, 1).at[bottom], zm)
    relay(G_MF, shard(0, 1).at[bottom], zm)
    relay(G_XB, shard(0, 1).at[bottom], xp)
    lax.fori_loop(4, 6, turn, 0)
    arrived(G_X, shard(1, 0), xp)
    relay(G_P1, shard(1, 0).at[bottom], zp)
    relay(G_M1, shard(1, 0).at[top], zm)
    pass_on(1, 0)
    arrived(G_PB, shard(0, 3).at[bottom], zp)
    pass_on(0, 3)
    arrived(G_MT, shard(0, 1).at[top], zm)
    pass_on(0, 1)
    lax.fori_loop(6, 9, turn, 0)
    from_sib(1, 0)
    project(1, 0)
    arrived(G_PF, shard(0, 2).at[top], zp)
    arrived(G_MF, shard(0, 2).at[bottom], zm)
    pass_on(0, 2)
    arrived(G_XA, shard(1, 3).at[top], xp)
    relay(G_P2, shard(1, 3).at[top], zp)
    from_sib(0, 3)
    project(0, 3)
    from_sib(0, 1)
    project(0, 1)
    lax.fori_loop(9, 11, turn, 0)
    arrived(G_XB, shard(1, 1).at[bottom], xp)
    relay(G_M2, shard(1, 1).at[bottom], zm)
    arrived(G_P1, shard(1, 3).at[bottom], zp)
    pass_on(1, 3)
    arrived(G_M1, shard(1, 1).at[top], zm)
    pass_on(1, 1)
    from_sib(0, 2)
    project(0, 2)
    lax.fori_loop(11, NF, turn, 0)
    from_sib(1, 3)
    project(1, 3)
    from_sib(1, 1)
    project(1, 1)
    arrived(G_P2, shard(1, 2).at[top], zp)
    arrived(G_M2, shard(1, 2).at[bottom], zm)
    pass_on(1, 2)
    from_sib(1, 2)
    project(1, 2)

    def dec_piece(k):
        to = peer(k)
        return msg(
            D_IN + k,
            dec.at[:, pl.ds(pl.multiple_of(to * ROWS, ROWS), ROWS)],
            dec_in.at[pl.ds(pl.multiple_of(f * DEC, DEC), DEC), :],
            (to, t),
        )

    def send_dec(k, carry):
        dec_piece(k).start()
        return carry

    lax.fori_loop(1, NF, send_dec, 0)
    own_dec = local(
        dec.at[:, pl.ds(pl.multiple_of(f * ROWS, ROWS), ROWS)],
        dec_in.at[pl.ds(pl.multiple_of(f * DEC, DEC), DEC), :],
        L_OWN,
    )
    own_dec.start()

    pb[...] = proj[...].astype(BF)
    load_og.wait()
    key_t[...] = pb[:, QC:QC + HD].T
    gk_acc[...] = jnp.zeros_like(gk_acc)
    gv_acc[...] = jnp.zeros_like(gv_acc)
    scale = 1.0 / math.sqrt(HD)
    width = TOK // 2

    def head(h, carry):
        at = pl.ds(pl.multiple_of(h * HD, HD), HD)
        for block in range(2):
            qs = pl.ds(block * width, width)
            seen = (block + 1) * width
            ks = pl.ds(0, seen)
            keys = pb[ks, pl.ds(QC, HD)]
            values = pb[ks, pl.ds(QC + HD, HD)]
            query = pb[qs, at]
            upstream = og[qs, at]
            scores = f32_dot_nt(keys, query) * scale + bias[ks, qs]
            expo = jnp.exp(scores - jnp.max(scores, 0, keepdims=True))
            probs = expo * (1.0 / jnp.sum(expo, 0, keepdims=True))
            dprob = f32_dot_nt(values, upstream)
            delta = jnp.sum(probs * dprob, 0, keepdims=True)
            dscore = (probs * (dprob - delta) * scale).astype(BF)
            gv_acc[ks, :] += f32_dot(probs.astype(BF), upstream)
            gk_acc[ks, :] += f32_dot(dscore, query)
            acts[qs, at] = f32_dot(key_t[:, ks], dscore).T.astype(BF)
        return carry

    lax.fori_loop(0, GROUPS, head, 0)
    acts[:, QC:QC + HD] = gk_acc[...].astype(BF)
    acts[:, QC + HD:] = gv_acc[...].astype(BF)

    def grad_block(slot):
        rows = tok_t[pl.ds(pl.multiple_of(slot * ROWS, ROWS), ROWS), :]
        return f32_dot(rows, acts[...])

    def block_of(i, dc):
        return ((xh + i // 4) % 2) * 8 + ((z + i % 4) % 4) * 2 + (c + dc) % 2

    def to_sib(i):
        return msg(R_SIB + i, sbs.at[i], acc.at[i], sib)

    def sib_block(k, carry):
        i = 7 - k
        sbs[i] = grad_block(block_of(i, 1)).astype(BF)
        to_sib(i).start()
        return carry

    def own_block(i, carry):
        block = grad_block(block_of(i, 0))
        arrived(R_SIB + i, acc.at[i], sib)
        acc[i] = (block + acc[i].astype(F32)).astype(BF)
        return carry

    def sums(dx, dz, part=None):
        ref = acc.at[place_of(dx, dz)]
        return ref if part is None else ref.at[part]

    def add(dst, *terms):
        total = dst[...].astype(F32)
        for x in terms:
            total = total + x[...].astype(F32)
        dst[...] = total.astype(BF)

    t_top, t_bottom = pl.ds(0, TOK // 2), pl.ds(TOK // 2, TOK // 2)

    def input_block(i, carry):
        rows = w[pl.ds(tid(i // 4, i % 4) * 2, 2)].reshape(2 * ROWS, COLS)
        part[i] = f32_dot_nt(acts[...], rows).astype(BF)
        return carry

    def send_near(dx):
        base, i = T_BASE + dx * 6, dx * 4
        send(base + T_PF, part.at[i + 2, t_top], tfp.at[dx], yp)
        send(base + T_MF, part.at[i + 2, t_bottom], tfm.at[dx], ym)
        send(base + T_PB, part.at[i + 1, t_bottom], tm.at[dx, t_bottom], yp)
        send(base + T_MB, part.at[i + 3, t_top], tp.at[dx, t_top], ym)

    def send_relayed(dx):
        base, i = T_BASE + dx * 6, dx * 4
        arrived(base + T_PF, tfp.at[dx], yp)
        add(part.at[i + 1, t_top], tfp.at[dx])
        send(base + T_PA, part.at[i + 1, t_top], tm.at[dx, t_top], yp)
        arrived(base + T_MF, tfm.at[dx], ym)
        add(part.at[i + 3, t_bottom], tfm.at[dx])
        send(base + T_MA, part.at[i + 3, t_bottom], tp.at[dx, t_bottom], ym)

    def ring_arrived(dx):
        base = T_BASE + dx * 6
        arrived(base + T_PB, tm.at[dx, t_bottom], yp)
        arrived(base + T_MB, tp.at[dx, t_top], ym)
        arrived(base + T_PA, tm.at[dx, t_top], yp)
        arrived(base + T_MA, tp.at[dx, t_bottom], ym)

    lax.fori_loop(0, 8, sib_block, 0)
    lax.fori_loop(4, 8, own_block, 0)
    send(R_X1T, sums(1, 2, top), rx1.at[top], xp)
    send(R_X1B, sums(1, 2, bottom), rx1.at[bottom], xp)
    send(R_PQ, sums(1, 1), qm, zp)
    send(R_MQ, sums(1, 3), qp, zm)
    lax.fori_loop(4, 8, input_block, 0)
    send_near(1)
    lax.fori_loop(0, 4, own_block, 0)
    lax.fori_loop(0, 4, input_block, 0)

    arrived(R_X1T, rx1.at[top], xp)
    add(sums(0, 2, top), rx1.at[top])
    send(R_PF, sums(0, 2, top), rfp, zp)
    send(R_PB, sums(0, 1, bottom), rm.at[bottom], zp)
    send(R_MB, sums(0, 3, top), rp.at[top], zm)
    send_relayed(1)
    send_near(0)
    arrived(R_X1B, rx1.at[bottom], xp)
    add(sums(0, 2, bottom), rx1.at[bottom])
    send(R_MF, sums(0, 2, bottom), rfm, zm)
    arrived(R_PQ, qm, zp)
    arrived(R_MQ, qp, zm)
    add(sums(1, 0), qm, qp)
    send(R_X2, sums(1, 0), rx0, xp)
    arrived(R_PF, rfp, zp)
    add(sums(0, 1, top), rfp)
    send(R_PA, sums(0, 1, top), rm.at[top], zp)
    arrived(R_MF, rfm, zm)
    add(sums(0, 3, bottom), rfm)
    send(R_MA, sums(0, 3, bottom), rp.at[bottom], zm)
    ring_arrived(1)
    add(part.at[4], tm.at[1], tp.at[1])
    send(T_X, part.at[4], tx, xt)
    send_relayed(0)

    arrived(R_PB, rm.at[bottom], zp)
    arrived(R_MB, rp.at[top], zm)
    arrived(R_PA, rm.at[top], zp)
    arrived(R_MA, rp.at[bottom], zm)
    arrived(R_X2, rx0, xp)
    total = sums(0, 0)[...].astype(F32) + rm[...].astype(F32) + rp[...].astype(F32) + rx0[...].astype(F32)
    grad = (total * (1.0 / NF)).astype(BF)
    gout[...] = grad
    stores = [
        local(gout.at[:, pl.ds(0, QC)], gq_o, L_GQ),
        local(gout.at[:, pl.ds(QC, HD)], gk_o, L_GK),
        local(gout.at[:, pl.ds(QC + HD, HD)], gv_o, L_GV),
    ]
    for m in stores:
        m.start()
    fresh = (own_w[...].astype(F32) - LEARN_RATE * grad.astype(F32)).astype(BF)

    def dec_arrived(k, carry):
        at = pl.ds(pl.multiple_of(peer(NF - k) * DEC, DEC), DEC)
        arrived(D_IN + k, dec_in.at[at, :], (peer(k), t))
        return carry

    lax.fori_loop(1, NF, dec_arrived, 0)
    own_dec.wait()
    dp[...] = f32_dot(dec_in[...], fresh).astype(BF)

    def dec_out_piece(k):
        to = peer(k)
        return msg(
            D_OUT + k,
            dp.at[pl.ds(pl.multiple_of(to * DEC, DEC), DEC), :],
            dpr.at[pl.ds(pl.multiple_of(f * DEC, DEC), DEC), :],
            (to, t),
        )

    def send_dec_out(k, carry):
        dec_out_piece(k).start()
        return carry

    lax.fori_loop(1, NF, send_dec_out, 0)
    own_rows = pl.ds(pl.multiple_of(f * DEC, DEC), DEC)
    own_part = local(dp.at[own_rows, :], dpr.at[own_rows, :], L_OWN2)
    own_part.start()
    load_kc.wait()
    load_vc.wait()

    def dec_out_arrived(k, carry):
        at = pl.ds(pl.multiple_of(peer(NF - k) * DEC, DEC), DEC)
        arrived(D_OUT + k, dpr.at[at, :], (peer(k), t))
        return carry

    lax.fori_loop(1, NF, dec_out_arrived, 0)
    own_part.wait()
    dsum = dpr[0:DEC, :].astype(F32)
    for k in range(1, NF):
        dsum = dsum + dpr[k * DEC:(k + 1) * DEC, :].astype(F32)
    dsum = dsum.astype(BF)

    dec_q = dsum[:, :QC].astype(F32)
    dec_k = dsum[:, QC:QC + HD]
    dec_v = dsum[:, QC + HD:]
    n_q = 2 * GROUPS
    place = lax.broadcasted_iota(jnp.int32, (n_q, CACHE), 1)
    new_col = lax.broadcasted_iota(jnp.int32, (n_q, DEC), 1)
    new_step = lax.broadcasted_iota(jnp.int32, (n_q, DEC), 0) % 2
    for r in range(DROWS):
        q = jnp.concatenate([dec_q[2 * r:2 * r + 2, g * HD:(g + 1) * HD] for g in range(GROUPS)], axis=0).astype(BF)
        older = jnp.where(place < lens[r], f32_dot_nt(q, kc[r]) * scale, MASKED)
        visible = (new_col // 2 == r) & (new_col % 2 <= new_step)
        newer = jnp.where(visible, f32_dot_nt(q, dec_k) * scale, MASKED)
        best = jnp.maximum(jnp.max(older, 1, keepdims=True), jnp.max(newer, 1, keepdims=True))
        exp_old = jnp.exp(older - best)
        exp_new = jnp.exp(newer - best)
        inv = 1.0 / (jnp.sum(exp_old, 1, keepdims=True) + jnp.sum(exp_new, 1, keepdims=True))
        mixed = f32_dot((exp_old * inv).astype(BF), vc[r]) + f32_dot((exp_new * inv).astype(BF), dec_v)
        for g in range(GROUPS):
            do_o[2 * r:2 * r + 2, g * HD:(g + 1) * HD] = mixed[2 * g:2 * g + 2, :]

    ring_arrived(0)
    arrived(T_X, tx, xt)
    total = part[0].astype(F32) + tm[0].astype(F32) + tp[0].astype(F32) + tx[...].astype(F32)
    ig[...] = total.astype(BF)
    store_ig = local(ig, ig_o, L_IG)
    store_ig.start()
    stores.append(store_ig)

    for m in sent:
        m.wait_send()

    def sent_small(k, carry):
        dec_piece(k).wait_send()
        dec_out_piece(k).wait_send()
        return carry

    lax.fori_loop(1, NF, sent_small, 0)

    def sent_sib(i, carry):
        to_sib(i).wait_send()
        return carry

    lax.fori_loop(0, 8, sent_sib, 0)
    for m in stores:
        m.wait()


def hand_out(*refs):
    given, out, held, sem = refs[:5], refs[5:10], refs[10:14], refs[14]
    into = [pltpu.make_async_copy(given[i], held[i], sem.at[i]) for i in range(4)]
    back = [pltpu.make_async_copy(held[i], out[i], sem.at[4 + i]) for i in range(4)]
    for m in into:
        m.start()
    for r in range(DROWS):
        out[4][r] = given[4][2 * r:2 * r + 2, :].astype(BF)
    for m, n in zip(into, back):
        m.wait()
        n.start()
    for n in back:
        n.wait()


def on_device(tokens, token_ids, out_grad, w_query, w_key, w_value, dec_states, cache_lens, key_cache, value_cache):
    anywhere = pl.BlockSpec(memory_space=pl.ANY)
    vmem = pl.BlockSpec(memory_space=pltpu.VMEM)

    def buf(*shape, dtype=BF):
        return pltpu.VMEM(shape, dtype)

    shapes = [(ROWS, QC), (ROWS, HD), (ROWS, HD), (TOK, FEAT), (DEC, QC)]
    results = pl.pallas_call(
        kernel,
        out_shape=[jax.ShapeDtypeStruct(s, F32 if s[0] == DEC else BF) for s in shapes],
        in_specs=[vmem, pl.BlockSpec(memory_space=pltpu.SMEM)] + [anywhere] * 8,
        out_specs=[anywhere] * 4 + [vmem],
        scratch_shapes=[
            buf(TOK, D), buf(D, TOK), buf(NF, ROWS, COLS), buf(TOK, COLS, dtype=F32), buf(TOK, COLS), buf(TOK, QC),
            buf(TOK, TOK, dtype=F32), buf(TOK, COLS), buf(HD, TOK), buf(TOK, HD, dtype=F32), buf(TOK, HD, dtype=F32),
            buf(8, ROWS, COLS), buf(8, ROWS, COLS),
            buf(ROWS, COLS), buf(ROWS, COLS), buf(ROWS, COLS), buf(ROWS, COLS), buf(ROWS, COLS), buf(ROWS, COLS),
            buf(HALF, COLS), buf(HALF, COLS),
            buf(8, TOK, FEAT), buf(2, TOK // 2, FEAT), buf(2, TOK // 2, FEAT), buf(2, TOK, FEAT), buf(2, TOK, FEAT),
            buf(TOK, FEAT), buf(TOK, FEAT), buf(ROWS, COLS),
            buf(DROWS, CACHE, HD), buf(DROWS, CACHE, HD),
            buf(DROWS, 2, D), buf(DEC, D, dtype=F32), buf(DEC, D), buf(NF * DEC, ROWS), buf(NF * DEC, COLS), buf(NF * DEC, COLS),
            pltpu.SemaphoreType.DMA((N_MSG,)), pltpu.SemaphoreType.DMA((N_MSG,)), pltpu.SemaphoreType.DMA((N_LOCAL,)),
        ],
        compiler_params=pltpu.CompilerParams(collective_id=0, has_side_effects=True, vmem_limit_bytes=60 << 20),
        cost_estimate=pl.CostEstimate(flops=13 * 10**9, bytes_accessed=16 * 10**6, transcendentals=2 * 10**6),
    )(
        token_ids.reshape(1, TOK), cache_lens, tokens, out_grad, w_query, w_key, w_value,
        dec_states, key_cache, value_cache,
    )
    shapes[4] = (DROWS, 2, QC)
    return tuple(
        pl.pallas_call(
            hand_out,
            out_shape=[jax.ShapeDtypeStruct(s, BF) for s in shapes],
            in_specs=[anywhere] * 4 + [vmem],
            out_specs=[anywhere] * 4 + [vmem],
            scratch_shapes=[buf(*s) for s in shapes[:4]] + [pltpu.SemaphoreType.DMA((8,))],
        )(*results)
    )


def solution(mesh):
    placed = (
        P("fsdp", None),
        P("fsdp"),
        P("fsdp", "tensor"),
        P("fsdp", "tensor"),
        P("fsdp", "tensor"),
        P("fsdp", "tensor"),
        P("fsdp", None, None),
        P("fsdp"),
        P("fsdp", None, "tensor"),
        P("fsdp", None, "tensor"),
    )
    return jax.shard_map(
        on_device,
        mesh=mesh,
        in_specs=placed,
        out_specs=(
            P("fsdp", "tensor"),
            P("fsdp", "tensor"),
            P("fsdp", "tensor"),
            P("fsdp", "tensor"),
            P("fsdp", None, "tensor"),
        ),
        check_vma=False,
    )
```

```python
import math

import jax
import jax.numpy as jnp
from jax import lax
from jax.experimental import pallas as pl
from jax.experimental.pallas import tpu as pltpu
from jax.sharding import PartitionSpec as P

MESH = pl.DeviceIdType.MESH
BF = jnp.bfloat16
F32 = jnp.float32

HD = 128
LEARN_RATE = 0.004
BOS_ID = 128000
MASKED = -1e30

TOK = 512
D = 4096
QC = 512
COLS = 768
ROWS = 256
HALF = ROWS // 2
GROUPS = QC // HD
NF = 16
FEAT = 512
DEC = 16
CACHE = 2048
DROWS = 8

G_SIB = 0
G_PT, G_PB, G_MT, G_MB, G_X, G_PF, G_MF, G_XA, G_XB, G_P1, G_M1, G_P2, G_M2 = range(8, 21)
R_SIB = 21
R_X1T, R_X1B, R_PQ, R_MQ, R_PB, R_MB, R_PF, R_MF, R_PA, R_MA, R_X2 = range(29, 40)
T_BASE = 40
T_PF, T_MF, T_PB, T_MB, T_PA, T_MA = range(6)
T_X = 52
D_IN = 53
D_OUT = 69
T_X2 = 85
N_MSG = 86

L_TOK, L_OG, L_WQ, L_WK, L_WV, L_DEC, L_KC, L_VC, L_OWN, L_GQ, L_GK, L_GV, L_IG, L_DO, L_OWN2, L_IDS, L_LENS, L_IG2 = range(18)
N_LOCAL = 18

NT = (((1,), (1,)), ((), ()))


def f32_dot(a, b):
    return jnp.dot(a, b, preferred_element_type=F32)


def f32_dot_nt(a, b):
    return lax.dot_general(a, b, NT, preferred_element_type=F32)


def kernel(
    ids_h, lens_h, tok_h, og_h, wq_h, wk_h, wv_h, dec_h, kc_h, vc_h,
    gq_o, gk_o, gv_o, ig_o, do_o,
    tok, tok_t, w, proj, pb, og, bias, acts, key_t, gk_acc, gv_acc,
    sbs, acc, rx1, rx0, rm, rp, qm, qp, rfm, rfp,
    part, tfm, tfp, tm, tp, tx, ig, gout,
    ids, lens, kc, vc, dec3, dec_f32, dec, dec_in, dp, dpr,
    ssem, rsem, lsem,
):
    f = lax.axis_index("fsdp")
    t = lax.axis_index("tensor")
    xh, z, c = f // 8, (f // 2) % 4, f % 2
    xl, y = t // 4, t % 4

    sense = 1 + 2 * c

    def fid(dx, dz, dc):
        return ((xh + dx) % 2) * 8 + ((z + sense * dz) % 4) * 2 + (c + dc) % 2

    def place_of(dx, dz):
        return dx * 4 + (sense * dz) % 4

    def tid(dx, dy):
        return ((xl + dx) % 2) * 4 + (y + dy) % 4

    sib = (fid(0, 0, 1), t)
    zp, zm, xp = (fid(0, 1, 0), t), (fid(0, 3, 0), t), (fid(1, 0, 0), t)
    yp, ym, xt = (f, tid(0, 1)), (f, tid(0, 3)), (f, tid(1, 0))

    def local(src, dst, i):
        return pltpu.make_async_copy(src, dst, lsem.at[i])

    sent = []

    def msg(i, src, dst, to):
        return pltpu.make_async_remote_copy(
            src_ref=src, dst_ref=dst, send_sem=ssem.at[i], recv_sem=rsem.at[i], device_id=to, device_id_type=MESH
        )

    def send(i, src, dst, to):
        m = msg(i, src, dst, to)
        m.start()
        sent.append(m)

    def arrived(i, ref, to):
        msg(i, ref, ref, to).wait_recv()

    def peer(k):
        return lax.rem(f + k, NF)

    near = (sib, zp, zm, xp, yp, ym, xt)
    barrier = pltpu.get_barrier_semaphore()
    for to in near:
        pl.semaphore_signal(barrier, inc=1, device_id=to, device_id_type=MESH)
    own_w = w.at[f]
    loads = [
        local(wq_h, own_w.at[:, pl.ds(0, QC)], L_WQ),
        local(wk_h, own_w.at[:, pl.ds(QC, HD)], L_WK),
        local(wv_h, own_w.at[:, pl.ds(QC + HD, HD)], L_WV),
    ]
    for m in loads:
        m.start()
    load_ids = local(ids_h, ids, L_IDS)
    load_ids.start()
    load_lens = local(lens_h, lens, L_LENS)
    load_lens.start()
    load_tok = local(tok_h, tok, L_TOK)
    load_tok.start()
    load_dec = local(dec_h, dec3, L_DEC)
    load_dec.start()
    load_og = local(og_h, og, L_OG)
    load_og.start()

    for m in loads:
        m.wait()
    pl.semaphore_wait(barrier, len(near))

    top, bottom = pl.ds(0, HALF), pl.ds(HALF, HALF)
    send(G_PT, own_w.at[top], own_w.at[top], zp)
    send(G_MB, own_w.at[bottom], own_w.at[bottom], zm)
    send(G_X, own_w, own_w, xp)
    send(G_PB, own_w.at[bottom], own_w.at[bottom], zp)
    send(G_MT, own_w.at[top], own_w.at[top], zm)
    send(G_SIB + place_of(0, 0), own_w, own_w, sib)

    load_kc = local(kc_h, kc, L_KC)
    load_vc = local(vc_h, vc, L_VC)
    load_kc.start()
    load_vc.start()

    load_ids.wait()
    bos = (ids[...] == BOS_ID).astype(F32)
    row = lax.broadcasted_iota(jnp.int32, (TOK, TOK), 0)
    col = lax.broadcasted_iota(jnp.int32, (TOK, TOK), 1)
    seg_row = f32_dot(jnp.broadcast_to(bos, (16, TOK)).astype(BF), (row <= col).astype(BF))
    seg_col = f32_dot_nt((col <= row).astype(BF), jnp.broadcast_to(bos, (HD, TOK)).astype(BF))
    seg_col = jnp.concatenate([seg_col] * (TOK // HD), axis=1)
    bias[...] = jnp.where((row <= col) & (seg_col == seg_row[0:1, :]), 0.0, MASKED)

    load_dec.wait()
    for r in range(DROWS):
        dec_f32[2 * r:2 * r + 2, :] = dec3[r].astype(F32)
    dec[...] = dec_f32[...].astype(BF)
    load_tok.wait()

    def turn(i, carry):
        at = pl.ds(pl.multiple_of(i * ROWS, ROWS), ROWS)
        tok_t[at, :] = tok[:, at].T
        return carry

    def project(dx, dz, first=False):
        chip = fid(dx, dz, 0) // 2
        at = pl.ds(pl.multiple_of(chip * 2 * ROWS, 2 * ROWS), 2 * ROWS)
        rows = w[pl.ds(chip * 2, 2)].reshape(2 * ROWS, COLS)
        term = f32_dot(tok[:, at], rows)
        proj[...] = term if first else proj[...] + term

    def shard(dx, dz, dc=0):
        return w.at[fid(dx, dz, dc)]

    def pass_on(dx, dz):
        send(G_SIB + place_of(dx, dz), shard(dx, dz), shard(dx, dz), sib)

    def from_sib(dx, dz):
        arrived(G_SIB + place_of(dx, dz), shard(dx, dz, 1), sib)

    def relay(i, ref, to):
        send(i, ref, ref, to)

    from_sib(0, 0)
    project(0, 0, True)
    lax.fori_loop(0, 4, turn, 0)

    arrived(G_PT, shard(0, 3).at[top], zp)
    relay(G_PF, shard(0, 3).at[top], zp)
    relay(G_XA, shard(0, 3).at[top], xp)
    arrived(G_MB, shard(0, 1).at[bottom], zm)
    relay(G_MF, shard(0, 1).at[bottom], zm)
    relay(G_XB, shard(0, 1).at[bottom], xp)
    lax.fori_loop(4, 6, turn, 0)
    arrived(G_X, shard(1, 0), xp)
    relay(G_P1, shard(1, 0).at[bottom], zp)
    relay(G_M1, shard(1, 0).at[top], zm)
    pass_on(1, 0)
    arrived(G_PB, shard(0, 3).at[bottom], zp)
    pass_on(0, 3)
    arrived(G_MT, shard(0, 1).at[top], zm)
    pass_on(0, 1)
    lax.fori_loop(6, 9, turn, 0)
    from_sib(1, 0)
    project(1, 0)
    arrived(G_PF, shard(0, 2).at[top], zp)
    arrived(G_MF, shard(0, 2).at[bottom], zm)
    pass_on(0, 2)
    arrived(G_XA, shard(1, 3).at[top], xp)
    relay(G_P2, shard(1, 3).at[top], zp)
    from_sib(0, 3)
    project(0, 3)
    from_sib(0, 1)
    project(0, 1)
    lax.fori_loop(9, 11, turn, 0)
    arrived(G_XB, shard(1, 1).at[bottom], xp)
    relay(G_M2, shard(1, 1).at[bottom], zm)
    arrived(G_P1, shard(1, 3).at[bottom], zp)
    pass_on(1, 3)
    arrived(G_M1, shard(1, 1).at[top], zm)
    pass_on(1, 1)
    from_sib(0, 2)
    project(0, 2)
    lax.fori_loop(11, NF, turn, 0)
    from_sib(1, 3)
    project(1, 3)
    from_sib(1, 1)
    project(1, 1)
    arrived(G_P2, shard(1, 2).at[top], zp)
    arrived(G_M2, shard(1, 2).at[bottom], zm)
    pass_on(1, 2)
    from_sib(1, 2)
    project(1, 2)

    def dec_piece(k):
        to = peer(k)
        return msg(
            D_IN + k,
            dec.at[:, pl.ds(pl.multiple_of(to * ROWS, ROWS), ROWS)],
            dec_in.at[pl.ds(pl.multiple_of(f * DEC, DEC), DEC), :],
            (to, t),
        )

    def send_dec(k, carry):
        dec_piece(k).start()
        return carry

    lax.fori_loop(1, NF, send_dec, 0)
    own_dec = local(
        dec.at[:, pl.ds(pl.multiple_of(f * ROWS, ROWS), ROWS)],
        dec_in.at[pl.ds(pl.multiple_of(f * DEC, DEC), DEC), :],
        L_OWN,
    )
    own_dec.start()

    pb[...] = proj[...].astype(BF)
    load_og.wait()
    key_t[...] = pb[:, QC:QC + HD].T
    gk_acc[...] = jnp.zeros_like(gk_acc)
    gv_acc[...] = jnp.zeros_like(gv_acc)
    scale = 1.0 / math.sqrt(HD)
    width = TOK // 2

    def head(h, carry):
        at = pl.ds(pl.multiple_of(h * HD, HD), HD)
        for block in range(2):
            qs = pl.ds(block * width, width)
            seen = (block + 1) * width
            ks = pl.ds(0, seen)
            keys = pb[ks, pl.ds(QC, HD)]
            values = pb[ks, pl.ds(QC + HD, HD)]
            query = pb[qs, at]
            upstream = og[qs, at]
            scores = f32_dot_nt(keys, query) * scale + bias[ks, qs]
            expo = jnp.exp(scores - jnp.max(scores, 0, keepdims=True))
            probs = expo * (1.0 / jnp.sum(expo, 0, keepdims=True))
            dprob = f32_dot_nt(values, upstream)
            delta = jnp.sum(probs * dprob, 0, keepdims=True)
            dscore = (probs * (dprob - delta) * scale).astype(BF)
            gv_acc[ks, :] += f32_dot(probs.astype(BF), upstream)
            gk_acc[ks, :] += f32_dot(dscore, query)
            acts[qs, at] = f32_dot(key_t[:, ks], dscore).T.astype(BF)
        return carry

    lax.fori_loop(0, GROUPS, head, 0, unroll=True)
    acts[:, QC:QC + HD] = gk_acc[...].astype(BF)
    acts[:, QC + HD:] = gv_acc[...].astype(BF)

    def grad_block(slot):
        rows = tok_t[pl.ds(pl.multiple_of(slot * ROWS, ROWS), ROWS), :]
        return f32_dot(rows, acts[...])

    def block_of(i, dc):
        return ((xh + i // 4) % 2) * 8 + ((z + i % 4) % 4) * 2 + (c + dc) % 2

    def to_sib(i):
        return msg(R_SIB + i, sbs.at[i], acc.at[i], sib)

    def sib_block(i):
        sbs[i] = grad_block(block_of(i, 1)).astype(BF)
        to_sib(i).start()

    def own_block(i):
        block = grad_block(block_of(i, 0))
        arrived(R_SIB + i, acc.at[i], sib)
        acc[i] = (block + acc[i].astype(F32)).astype(BF)

    def sums(dx, dz, part=None):
        ref = acc.at[place_of(dx, dz)]
        return ref if part is None else ref.at[part]

    def add(dst, *terms):
        total = dst[...].astype(F32)
        for x in terms:
            total = total + x[...].astype(F32)
        dst[...] = total.astype(BF)

    t_top, t_bottom = pl.ds(0, TOK // 2), pl.ds(TOK // 2, TOK // 2)

    def input_block(i):
        rows = w[pl.ds(tid(i // 4, i % 4) * 2, 2)].reshape(2 * ROWS, COLS)
        part[i] = f32_dot_nt(acts[...], rows).astype(BF)

    def send_far(dx):
        base, i = T_BASE + dx * 6, dx * 4
        send(base + T_PF, part.at[i + 2, t_top], tfp.at[dx], yp)
        send(base + T_MF, part.at[i + 2, t_bottom], tfm.at[dx], ym)

    def send_near(dx):
        base, i = T_BASE + dx * 6, dx * 4
        send(base + T_PB, part.at[i + 1, t_bottom], tm.at[dx, t_bottom], yp)
        send(base + T_MB, part.at[i + 3, t_top], tp.at[dx, t_top], ym)

    def send_relayed(dx):
        base, i = T_BASE + dx * 6, dx * 4
        arrived(base + T_PF, tfp.at[dx], yp)
        add(part.at[i + 1, t_top], tfp.at[dx])
        send(base + T_PA, part.at[i + 1, t_top], tm.at[dx, t_top], yp)
        arrived(base + T_MF, tfm.at[dx], ym)
        add(part.at[i + 3, t_bottom], tfm.at[dx])
        send(base + T_MA, part.at[i + 3, t_bottom], tp.at[dx, t_bottom], ym)

    def ring_arrived(dx):
        base = T_BASE + dx * 6
        arrived(base + T_PB, tm.at[dx, t_bottom], yp)
        arrived(base + T_MB, tp.at[dx, t_top], ym)
        arrived(base + T_PA, tm.at[dx, t_top], yp)
        arrived(base + T_MA, tp.at[dx, t_bottom], ym)

    input_block(6)
    send_far(1)
    input_block(5)
    input_block(7)
    send_near(1)
    for i in (6, 5, 7, 4):
        sib_block(i)
    own_block(6)
    send(R_X1T, sums(1, 2, top), rx1.at[top], xp)
    send(R_X1B, sums(1, 2, bottom), rx1.at[bottom], xp)
    own_block(5)
    own_block(7)
    send(R_PQ, sums(1, 1), qm, zp)
    send(R_MQ, sums(1, 3), qp, zm)
    own_block(4)
    for i in (2, 1, 3, 0):
        sib_block(i)
    for i in (2, 1, 3):
        input_block(i)

    send_relayed(1)
    send_far(0)
    send_near(0)
    for i in (2, 1, 3, 0):
        own_block(i)
    arrived(R_X1T, rx1.at[top], xp)
    add(sums(0, 2, top), rx1.at[top])
    send(R_PF, sums(0, 2, top), rfp, zp)
    send(R_PB, sums(0, 1, bottom), rm.at[bottom], zp)
    send(R_MB, sums(0, 3, top), rp.at[top], zm)
    arrived(R_X1B, rx1.at[bottom], xp)
    add(sums(0, 2, bottom), rx1.at[bottom])
    send(R_MF, sums(0, 2, bottom), rfm, zm)
    input_block(4)
    arrived(R_PQ, qm, zp)
    arrived(R_MQ, qp, zm)
    add(sums(1, 0), qm, qp)
    send(R_X2, sums(1, 0), rx0, xp)
    input_block(0)
    arrived(R_PF, rfp, zp)
    add(sums(0, 1, top), rfp)
    send(R_PA, sums(0, 1, top), rm.at[top], zp)
    ring_arrived(1)
    add(part.at[4], tm.at[1], tp.at[1])
    send(T_X, part.at[4, t_top], tx.at[t_top], xt)
    arrived(R_MF, rfm, zm)
    add(sums(0, 3, bottom), rfm)
    send(R_MA, sums(0, 3, bottom), rp.at[bottom], zm)
    send_relayed(0)

    arrived(R_PB, rm.at[bottom], zp)
    arrived(R_MB, rp.at[top], zm)
    arrived(R_PA, rm.at[top], zp)
    arrived(R_MA, rp.at[bottom], zm)
    arrived(R_X2, rx0, xp)
    total = sums(0, 0)[...].astype(F32) + rm[...].astype(F32) + rp[...].astype(F32) + rx0[...].astype(F32)
    grad = (total * (1.0 / NF)).astype(BF)
    gout[...] = grad
    stores = [
        local(gout.at[:, pl.ds(0, QC)], gq_o, L_GQ),
        local(gout.at[:, pl.ds(QC, HD)], gk_o, L_GK),
        local(gout.at[:, pl.ds(QC + HD, HD)], gv_o, L_GV),
    ]
    for m in stores:
        m.start()
    fresh = (own_w[...].astype(F32) - LEARN_RATE * grad.astype(F32)).astype(BF)

    def dec_arrived(k, carry):
        at = pl.ds(pl.multiple_of(peer(NF - k) * DEC, DEC), DEC)
        arrived(D_IN + k, dec_in.at[at, :], (peer(k), t))
        return carry

    lax.fori_loop(1, NF, dec_arrived, 0)
    own_dec.wait()
    dp[...] = f32_dot(dec_in[...], fresh).astype(BF)

    def dec_out_piece(k):
        to = peer(k)
        return msg(
            D_OUT + k,
            dp.at[pl.ds(pl.multiple_of(to * DEC, DEC), DEC), :],
            dpr.at[pl.ds(pl.multiple_of(f * DEC, DEC), DEC), :],
            (to, t),
        )

    def send_dec_out(k, carry):
        dec_out_piece(k).start()
        return carry

    lax.fori_loop(1, NF, send_dec_out, 0)
    send(T_X2, part.at[4, t_bottom], tx.at[t_bottom], xt)
    own_rows = pl.ds(pl.multiple_of(f * DEC, DEC), DEC)
    own_part = local(dp.at[own_rows, :], dpr.at[own_rows, :], L_OWN2)
    own_part.start()
    def input_half(rows, i):
        total = part[0, rows].astype(F32) + tm[0, rows].astype(F32) + tp[0, rows].astype(F32) + tx[rows, :].astype(F32)
        ig[rows, :] = total.astype(BF)
        store = local(ig.at[rows], ig_o.at[rows], i)
        store.start()
        stores.append(store)

    ring_arrived(0)
    arrived(T_X, tx.at[t_top], xt)
    input_half(t_top, L_IG)
    load_lens.wait()
    load_kc.wait()
    load_vc.wait()

    def dec_out_arrived(k, carry):
        at = pl.ds(pl.multiple_of(peer(NF - k) * DEC, DEC), DEC)
        arrived(D_OUT + k, dpr.at[at, :], (peer(k), t))
        return carry

    lax.fori_loop(1, NF, dec_out_arrived, 0)
    own_part.wait()
    dsum = dpr[0:DEC, :].astype(F32)
    for k in range(1, NF):
        dsum = dsum + dpr[k * DEC:(k + 1) * DEC, :].astype(F32)
    dsum = dsum.astype(BF)

    dec_q = dsum[:, :QC].astype(F32)
    dec_k = dsum[:, QC:QC + HD]
    dec_v = dsum[:, QC + HD:]
    n_q = 2 * GROUPS
    place = lax.broadcasted_iota(jnp.int32, (n_q, CACHE), 1)
    new_col = lax.broadcasted_iota(jnp.int32, (n_q, DEC), 1)
    new_step = lax.broadcasted_iota(jnp.int32, (n_q, DEC), 0) % 2
    for r in range(DROWS):
        q = jnp.concatenate([dec_q[2 * r:2 * r + 2, g * HD:(g + 1) * HD] for g in range(GROUPS)], axis=0).astype(BF)
        older = jnp.where(place < lens[r], f32_dot_nt(q, kc[r]) * scale, MASKED)
        visible = (new_col // 2 == r) & (new_col % 2 <= new_step)
        newer = jnp.where(visible, f32_dot_nt(q, dec_k) * scale, MASKED)
        best = jnp.maximum(jnp.max(older, 1, keepdims=True), jnp.max(newer, 1, keepdims=True))
        exp_old = jnp.exp(older - best)
        exp_new = jnp.exp(newer - best)
        inv = 1.0 / (jnp.sum(exp_old, 1, keepdims=True) + jnp.sum(exp_new, 1, keepdims=True))
        mixed = f32_dot((exp_old * inv).astype(BF), vc[r]) + f32_dot((exp_new * inv).astype(BF), dec_v)
        for g in range(GROUPS):
            do_o[2 * r:2 * r + 2, g * HD:(g + 1) * HD] = mixed[2 * g:2 * g + 2, :]

    arrived(T_X2, tx.at[t_bottom], xt)
    input_half(t_bottom, L_IG2)
    for m in sent:
        m.wait_send()

    def sent_small(k, carry):
        dec_piece(k).wait_send()
        dec_out_piece(k).wait_send()
        return carry

    lax.fori_loop(1, NF, sent_small, 0)

    def sent_sib(i, carry):
        to_sib(i).wait_send()
        return carry

    lax.fori_loop(0, 8, sent_sib, 0)
    for m in stores:
        m.wait()


def hand_out(*refs):
    given, out, held, sem = refs[:5], refs[5:10], refs[10:14], refs[14]
    into = [pltpu.make_async_copy(given[i], held[i], sem.at[i]) for i in range(4)]
    back = [pltpu.make_async_copy(held[i], out[i], sem.at[4 + i]) for i in range(4)]
    for m in into:
        m.start()
    for r in range(DROWS):
        out[4][r] = given[4][2 * r:2 * r + 2, :].astype(BF)
    for m, n in zip(into, back):
        m.wait()
        n.start()
    for n in back:
        n.wait()


def on_device(tokens, token_ids, out_grad, w_query, w_key, w_value, dec_states, cache_lens, key_cache, value_cache):
    anywhere = pl.BlockSpec(memory_space=pl.ANY)
    vmem = pl.BlockSpec(memory_space=pltpu.VMEM)

    def buf(*shape, dtype=BF):
        return pltpu.VMEM(shape, dtype)

    shapes = [(ROWS, QC), (ROWS, HD), (ROWS, HD), (TOK, FEAT), (DEC, QC)]
    results = pl.pallas_call(
        kernel,
        out_shape=[jax.ShapeDtypeStruct(s, F32 if s[0] == DEC else BF) for s in shapes],
        in_specs=[anywhere] * 10,
        out_specs=[anywhere] * 4 + [vmem],
        scratch_shapes=[
            buf(TOK, D), buf(D, TOK), buf(NF, ROWS, COLS), buf(TOK, COLS, dtype=F32), buf(TOK, COLS), buf(TOK, QC),
            buf(TOK, TOK, dtype=F32), buf(TOK, COLS), buf(HD, TOK), buf(TOK, HD, dtype=F32), buf(TOK, HD, dtype=F32),
            buf(8, ROWS, COLS), buf(8, ROWS, COLS),
            buf(ROWS, COLS), buf(ROWS, COLS), buf(ROWS, COLS), buf(ROWS, COLS), buf(ROWS, COLS), buf(ROWS, COLS),
            buf(HALF, COLS), buf(HALF, COLS),
            buf(8, TOK, FEAT), buf(2, TOK // 2, FEAT), buf(2, TOK // 2, FEAT), buf(2, TOK, FEAT), buf(2, TOK, FEAT),
            buf(TOK, FEAT), buf(TOK, FEAT), buf(ROWS, COLS),
            buf(1, TOK, dtype=jnp.int32), pltpu.SMEM((DROWS,), jnp.int32),
            buf(DROWS, CACHE, HD), buf(DROWS, CACHE, HD),
            buf(DROWS, 2, D), buf(DEC, D, dtype=F32), buf(DEC, D), buf(NF * DEC, ROWS), buf(NF * DEC, COLS), buf(NF * DEC, COLS),
            pltpu.SemaphoreType.DMA((N_MSG,)), pltpu.SemaphoreType.DMA((N_MSG,)), pltpu.SemaphoreType.DMA((N_LOCAL,)),
        ],
        compiler_params=pltpu.CompilerParams(collective_id=0, has_side_effects=True, vmem_limit_bytes=60 << 20),
        cost_estimate=pl.CostEstimate(flops=13 * 10**9, bytes_accessed=16 * 10**6, transcendentals=2 * 10**6),
    )(
        token_ids.reshape(1, TOK), cache_lens, tokens, out_grad, w_query, w_key, w_value,
        dec_states, key_cache, value_cache,
    )
    shapes[4] = (DROWS, 2, QC)
    return tuple(
        pl.pallas_call(
            hand_out,
            out_shape=[jax.ShapeDtypeStruct(s, BF) for s in shapes],
            in_specs=[anywhere] * 4 + [vmem],
            out_specs=[anywhere] * 4 + [vmem],
            scratch_shapes=[buf(*s) for s in shapes[:4]] + [pltpu.SemaphoreType.DMA((8,))],
        )(*results)
    )


def solution(mesh):
    placed = (
        P("fsdp", None),
        P("fsdp"),
        P("fsdp", "tensor"),
        P("fsdp", "tensor"),
        P("fsdp", "tensor"),
        P("fsdp", "tensor"),
        P("fsdp", None, None),
        P("fsdp"),
        P("fsdp", None, "tensor"),
        P("fsdp", None, "tensor"),
    )
    return jax.shard_map(
        on_device,
        mesh=mesh,
        in_specs=placed,
        out_specs=(
            P("fsdp", "tensor"),
            P("fsdp", "tensor"),
            P("fsdp", "tensor"),
            P("fsdp", "tensor"),
            P("fsdp", None, "tensor"),
        ),
        check_vma=False,
    )
```

```python
import math

import jax
import jax.numpy as jnp
from jax import lax
from jax.experimental import pallas as pl
from jax.experimental.pallas import tpu as pltpu
from jax.sharding import PartitionSpec as P

MESH = pl.DeviceIdType.MESH
BF = jnp.bfloat16
F32 = jnp.float32

HD = 128
LEARN_RATE = 0.004
BOS_ID = 128000
MASKED = -1e30

TOK = 512
D = 4096
QC = 512
COLS = 768
ROWS = 256
HALF = ROWS // 2
GROUPS = QC // HD
NF = 16
FEAT = 512
DEC = 16
CACHE = 2048
DROWS = 8

G_SIB = 0
G_PT, G_PB, G_MT, G_MB, G_X, G_PF, G_MF, G_XA, G_XB, G_P1, G_M1, G_P2, G_M2 = range(8, 21)
R_SIB = 21
R_X1T, R_X1B, R_PQ, R_MQ, R_PB, R_MB, R_PF, R_MF, R_PA, R_MA, R_X2 = range(29, 40)
T_BASE = 40
T_PF, T_MF, T_PB, T_MB, T_PA, T_MA = range(6)
T_X = 52
D_IN = 53
D_OUT = 69
T_X2 = 85
N_MSG = 86

L_TOK, L_OG, L_WQ, L_WK, L_WV, L_DEC, L_KC, L_VC, L_OWN, L_GQ, L_GK, L_GV, L_IG, L_DO, L_OWN2, L_IDS, L_LENS, L_IG2 = range(18)
N_LOCAL = 18

NT = (((1,), (1,)), ((), ()))


def f32_dot(a, b):
    return jnp.dot(a, b, preferred_element_type=F32)


def f32_dot_nt(a, b):
    return lax.dot_general(a, b, NT, preferred_element_type=F32)


def kernel(
    ids_h, lens_h, tok_h, og_h, wq_h, wk_h, wv_h, dec_h, kc_h, vc_h,
    gq_o, gk_o, gv_o, ig_o, do_o,
    tok, tok_t, w, proj, pb, og, bias, acts, key_t, gk_acc, gv_acc,
    sbs, acc, rx1, rx0, rm, rp, qm, qp, rfm, rfp,
    part, tfm, tfp, tm, tp, tx, ig, gout,
    ids, lens, kc, vc, dec3, dec_f32, dec, dec_in, dp, dpr, dout, older,
    ssem, rsem, lsem,
):
    f = lax.axis_index("fsdp")
    t = lax.axis_index("tensor")
    xh, z, c = f // 8, (f // 2) % 4, f % 2
    xl, y = t // 4, t % 4

    sense = 1 + 2 * c

    def fid(dx, dz, dc):
        return ((xh + dx) % 2) * 8 + ((z + sense * dz) % 4) * 2 + (c + dc) % 2

    def place_of(dx, dz):
        return dx * 4 + (sense * dz) % 4

    def tid(dx, dy):
        return ((xl + dx) % 2) * 4 + (y + dy) % 4

    sib = (fid(0, 0, 1), t)
    zp, zm, xp = (fid(0, 1, 0), t), (fid(0, 3, 0), t), (fid(1, 0, 0), t)
    yp, ym, xt = (f, tid(0, 1)), (f, tid(0, 3)), (f, tid(1, 0))

    def local(src, dst, i):
        return pltpu.make_async_copy(src, dst, lsem.at[i])

    sent = []

    def msg(i, src, dst, to):
        return pltpu.make_async_remote_copy(
            src_ref=src, dst_ref=dst, send_sem=ssem.at[i], recv_sem=rsem.at[i], device_id=to, device_id_type=MESH
        )

    def send(i, src, dst, to):
        m = msg(i, src, dst, to)
        m.start()
        sent.append(m)

    def arrived(i, ref, to):
        msg(i, ref, ref, to).wait_recv()

    def peer(k):
        return lax.rem(f + k, NF)

    near = (sib, zp, zm, xp, yp, ym, xt)
    barrier = pltpu.get_barrier_semaphore()
    for to in near:
        pl.semaphore_signal(barrier, inc=1, device_id=to, device_id_type=MESH)
    own_w = w.at[f]
    loads = [
        local(wq_h, own_w.at[:, pl.ds(0, QC)], L_WQ),
        local(wk_h, own_w.at[:, pl.ds(QC, HD)], L_WK),
        local(wv_h, own_w.at[:, pl.ds(QC + HD, HD)], L_WV),
    ]
    for m in loads:
        m.start()
    load_ids = local(ids_h, ids, L_IDS)
    load_ids.start()
    load_lens = local(lens_h, lens, L_LENS)
    load_lens.start()
    load_tok = local(tok_h, tok, L_TOK)
    load_tok.start()
    load_dec = local(dec_h, dec3, L_DEC)
    load_dec.start()
    load_og = local(og_h, og, L_OG)
    load_og.start()

    for m in loads:
        m.wait()
    pl.semaphore_wait(barrier, len(near))

    top, bottom = pl.ds(0, HALF), pl.ds(HALF, HALF)
    send(G_PT, own_w.at[top], own_w.at[top], zp)
    send(G_MB, own_w.at[bottom], own_w.at[bottom], zm)
    send(G_X, own_w, own_w, xp)
    send(G_PB, own_w.at[bottom], own_w.at[bottom], zp)
    send(G_MT, own_w.at[top], own_w.at[top], zm)
    send(G_SIB + place_of(0, 0), own_w, own_w, sib)

    load_kc = local(kc_h, kc, L_KC)
    load_vc = local(vc_h, vc, L_VC)
    load_kc.start()
    load_vc.start()

    load_ids.wait()
    bos = (ids[...] == BOS_ID).astype(F32)
    row = lax.broadcasted_iota(jnp.int32, (TOK, TOK), 0)
    col = lax.broadcasted_iota(jnp.int32, (TOK, TOK), 1)
    seg_row = f32_dot(jnp.broadcast_to(bos, (16, TOK)).astype(BF), (row <= col).astype(BF))
    seg_col = f32_dot_nt((col <= row).astype(BF), jnp.broadcast_to(bos, (HD, TOK)).astype(BF))
    seg_col = jnp.concatenate([seg_col] * (TOK // HD), axis=1)
    bias[...] = jnp.where((row <= col) & (seg_col == seg_row[0:1, :]), 0.0, MASKED)

    load_dec.wait()
    for r in range(DROWS):
        dec_f32[2 * r:2 * r + 2, :] = dec3[r].astype(F32)
    dec[...] = dec_f32[...].astype(BF)
    load_tok.wait()

    def turn(i, carry):
        at = pl.ds(pl.multiple_of(i * ROWS, ROWS), ROWS)
        tok_t[at, :] = tok[:, at].T
        return carry

    def project(dx, dz, first=False):
        chip = fid(dx, dz, 0) // 2
        at = pl.ds(pl.multiple_of(chip * 2 * ROWS, 2 * ROWS), 2 * ROWS)
        rows = w[pl.ds(chip * 2, 2)].reshape(2 * ROWS, COLS)
        term = f32_dot(tok[:, at], rows)
        proj[...] = term if first else proj[...] + term

    def shard(dx, dz, dc=0):
        return w.at[fid(dx, dz, dc)]

    def pass_on(dx, dz):
        send(G_SIB + place_of(dx, dz), shard(dx, dz), shard(dx, dz), sib)

    def from_sib(dx, dz):
        arrived(G_SIB + place_of(dx, dz), shard(dx, dz, 1), sib)

    def relay(i, ref, to):
        send(i, ref, ref, to)

    from_sib(0, 0)
    project(0, 0, True)
    lax.fori_loop(0, 4, turn, 0)

    arrived(G_PT, shard(0, 3).at[top], zp)
    relay(G_PF, shard(0, 3).at[top], zp)
    relay(G_XA, shard(0, 3).at[top], xp)
    arrived(G_MB, shard(0, 1).at[bottom], zm)
    relay(G_MF, shard(0, 1).at[bottom], zm)
    relay(G_XB, shard(0, 1).at[bottom], xp)
    lax.fori_loop(4, 6, turn, 0)
    arrived(G_X, shard(1, 0), xp)
    relay(G_P1, shard(1, 0).at[bottom], zp)
    relay(G_M1, shard(1, 0).at[top], zm)
    pass_on(1, 0)
    arrived(G_PB, shard(0, 3).at[bottom], zp)
    pass_on(0, 3)
    arrived(G_MT, shard(0, 1).at[top], zm)
    pass_on(0, 1)
    lax.fori_loop(6, 9, turn, 0)
    from_sib(1, 0)
    project(1, 0)
    arrived(G_PF, shard(0, 2).at[top], zp)
    arrived(G_MF, shard(0, 2).at[bottom], zm)
    pass_on(0, 2)
    arrived(G_XA, shard(1, 3).at[top], xp)
    relay(G_P2, shard(1, 3).at[top], zp)
    from_sib(0, 3)
    project(0, 3)
    from_sib(0, 1)
    project(0, 1)
    lax.fori_loop(9, 11, turn, 0)
    arrived(G_XB, shard(1, 1).at[bottom], xp)
    relay(G_M2, shard(1, 1).at[bottom], zm)
    arrived(G_P1, shard(1, 3).at[bottom], zp)
    pass_on(1, 3)
    arrived(G_M1, shard(1, 1).at[top], zm)
    pass_on(1, 1)
    from_sib(0, 2)
    project(0, 2)
    lax.fori_loop(11, NF, turn, 0)
    from_sib(1, 3)
    project(1, 3)
    from_sib(1, 1)
    project(1, 1)
    arrived(G_P2, shard(1, 2).at[top], zp)
    arrived(G_M2, shard(1, 2).at[bottom], zm)
    pass_on(1, 2)
    from_sib(1, 2)
    project(1, 2)

    def dec_piece(k):
        to = peer(k)
        return msg(
            D_IN + k,
            dec.at[:, pl.ds(pl.multiple_of(to * ROWS, ROWS), ROWS)],
            dec_in.at[pl.ds(pl.multiple_of(f * DEC, DEC), DEC), :],
            (to, t),
        )

    def send_dec(k, carry):
        dec_piece(k).start()
        return carry

    lax.fori_loop(1, NF, send_dec, 0)
    own_dec = local(
        dec.at[:, pl.ds(pl.multiple_of(f * ROWS, ROWS), ROWS)],
        dec_in.at[pl.ds(pl.multiple_of(f * DEC, DEC), DEC), :],
        L_OWN,
    )
    own_dec.start()

    pb[...] = proj[...].astype(BF)
    load_og.wait()
    key_t[...] = pb[:, QC:QC + HD].T
    gk_acc[...] = jnp.zeros_like(gk_acc)
    gv_acc[...] = jnp.zeros_like(gv_acc)
    scale = 1.0 / math.sqrt(HD)
    width = TOK // 2

    def head(h, carry):
        at = pl.ds(pl.multiple_of(h * HD, HD), HD)
        for block in range(2):
            qs = pl.ds(block * width, width)
            seen = (block + 1) * width
            ks = pl.ds(0, seen)
            keys = pb[ks, pl.ds(QC, HD)]
            values = pb[ks, pl.ds(QC + HD, HD)]
            query = pb[qs, at]
            upstream = og[qs, at]
            scores = f32_dot_nt(keys, query) * scale + bias[ks, qs]
            expo = jnp.exp(scores - jnp.max(scores, 0, keepdims=True))
            probs = expo * (1.0 / jnp.sum(expo, 0, keepdims=True))
            dprob = f32_dot_nt(values, upstream)
            delta = jnp.sum(probs * dprob, 0, keepdims=True)
            dscore = (probs * (dprob - delta) * scale).astype(BF)
            gv_acc[ks, :] += f32_dot(probs.astype(BF), upstream)
            gk_acc[ks, :] += f32_dot(dscore, query)
            acts[qs, at] = f32_dot(key_t[:, ks], dscore).T.astype(BF)
        return carry

    lax.fori_loop(0, GROUPS, head, 0, unroll=True)
    acts[:, QC:QC + HD] = gk_acc[...].astype(BF)
    acts[:, QC + HD:] = gv_acc[...].astype(BF)

    def grad_block(slot):
        rows = tok_t[pl.ds(pl.multiple_of(slot * ROWS, ROWS), ROWS), :]
        return f32_dot(rows, acts[...])

    def block_of(i, dc):
        return ((xh + i // 4) % 2) * 8 + ((z + i % 4) % 4) * 2 + (c + dc) % 2

    def to_sib(i):
        return msg(R_SIB + i, sbs.at[i], acc.at[i], sib)

    def sib_block(i):
        sbs[i] = grad_block(block_of(i, 1)).astype(BF)
        to_sib(i).start()

    def own_block(i):
        block = grad_block(block_of(i, 0))
        arrived(R_SIB + i, acc.at[i], sib)
        acc[i] = (block + acc[i].astype(F32)).astype(BF)

    def sums(dx, dz, part=None):
        ref = acc.at[place_of(dx, dz)]
        return ref if part is None else ref.at[part]

    def add(dst, *terms):
        total = dst[...].astype(F32)
        for x in terms:
            total = total + x[...].astype(F32)
        dst[...] = total.astype(BF)

    t_top, t_bottom = pl.ds(0, TOK // 2), pl.ds(TOK // 2, TOK // 2)

    def input_block(i):
        rows = w[pl.ds(tid(i // 4, i % 4) * 2, 2)].reshape(2 * ROWS, COLS)
        part[i] = f32_dot_nt(acts[...], rows).astype(BF)

    def send_far(dx):
        base, i = T_BASE + dx * 6, dx * 4
        send(base + T_PF, part.at[i + 2, t_top], tfp.at[dx], yp)
        send(base + T_MF, part.at[i + 2, t_bottom], tfm.at[dx], ym)

    def send_near(dx):
        base, i = T_BASE + dx * 6, dx * 4
        send(base + T_PB, part.at[i + 1, t_bottom], tm.at[dx, t_bottom], yp)
        send(base + T_MB, part.at[i + 3, t_top], tp.at[dx, t_top], ym)

    def send_relayed(dx):
        base, i = T_BASE + dx * 6, dx * 4
        arrived(base + T_PF, tfp.at[dx], yp)
        add(part.at[i + 1, t_top], tfp.at[dx])
        send(base + T_PA, part.at[i + 1, t_top], tm.at[dx, t_top], yp)
        arrived(base + T_MF, tfm.at[dx], ym)
        add(part.at[i + 3, t_bottom], tfm.at[dx])
        send(base + T_MA, part.at[i + 3, t_bottom], tp.at[dx, t_bottom], ym)

    def ring_arrived(dx):
        base = T_BASE + dx * 6
        arrived(base + T_PB, tm.at[dx, t_bottom], yp)
        arrived(base + T_MB, tp.at[dx, t_top], ym)
        arrived(base + T_PA, tm.at[dx, t_top], yp)
        arrived(base + T_MA, tp.at[dx, t_bottom], ym)

    input_block(6)
    send_far(1)
    for i in (6, 5, 7):
        sib_block(i)
    own_block(6)
    send(R_X1T, sums(1, 2, top), rx1.at[top], xp)
    send(R_X1B, sums(1, 2, bottom), rx1.at[bottom], xp)
    own_block(5)
    own_block(7)
    send(R_PQ, sums(1, 1), qm, zp)
    send(R_MQ, sums(1, 3), qp, zm)
    input_block(5)
    input_block(7)
    send_near(1)
    for i in (2, 1, 3, 4, 0):
        sib_block(i)
    input_block(2)
    input_block(1)
    input_block(3)

    send_relayed(1)
    send_far(0)
    send_near(0)
    for i in (2, 1, 3, 4, 0):
        own_block(i)
    arrived(R_X1T, rx1.at[top], xp)
    add(sums(0, 2, top), rx1.at[top])
    send(R_PF, sums(0, 2, top), rfp, zp)
    send(R_PB, sums(0, 1, bottom), rm.at[bottom], zp)
    send(R_MB, sums(0, 3, top), rp.at[top], zm)
    arrived(R_X1B, rx1.at[bottom], xp)
    add(sums(0, 2, bottom), rx1.at[bottom])
    send(R_MF, sums(0, 2, bottom), rfm, zm)
    input_block(4)
    arrived(R_PQ, qm, zp)
    arrived(R_MQ, qp, zm)
    add(sums(1, 0), qm, qp)
    send(R_X2, sums(1, 0), rx0, xp)
    input_block(0)
    arrived(R_PF, rfp, zp)
    add(sums(0, 1, top), rfp)
    send(R_PA, sums(0, 1, top), rm.at[top], zp)
    ring_arrived(1)
    add(part.at[4], tm.at[1], tp.at[1])
    send(T_X, part.at[4, t_top], tx.at[t_top], xt)
    arrived(R_MF, rfm, zm)
    add(sums(0, 3, bottom), rfm)
    send(R_MA, sums(0, 3, bottom), rp.at[bottom], zm)
    send_relayed(0)

    arrived(R_PB, rm.at[bottom], zp)
    arrived(R_MB, rp.at[top], zm)
    arrived(R_PA, rm.at[top], zp)
    arrived(R_MA, rp.at[bottom], zm)
    arrived(R_X2, rx0, xp)
    total = sums(0, 0)[...].astype(F32) + rm[...].astype(F32) + rp[...].astype(F32) + rx0[...].astype(F32)
    grad = (total * (1.0 / NF)).astype(BF)
    gout[...] = grad
    stores = [
        local(gout.at[:, pl.ds(0, QC)], gq_o, L_GQ),
        local(gout.at[:, pl.ds(QC, HD)], gk_o, L_GK),
        local(gout.at[:, pl.ds(QC + HD, HD)], gv_o, L_GV),
    ]
    for m in stores:
        m.start()
    fresh = (own_w[...].astype(F32) - LEARN_RATE * grad.astype(F32)).astype(BF)

    def dec_arrived(k, carry):
        at = pl.ds(pl.multiple_of(peer(NF - k) * DEC, DEC), DEC)
        arrived(D_IN + k, dec_in.at[at, :], (peer(k), t))
        return carry

    lax.fori_loop(1, NF, dec_arrived, 0)
    own_dec.wait()
    dp[...] = f32_dot(dec_in[...], fresh).astype(BF)

    def dec_out_piece(k):
        to = peer(k)
        return msg(
            D_OUT + k,
            dp.at[pl.ds(pl.multiple_of(to * DEC, DEC), DEC), :],
            dpr.at[pl.ds(pl.multiple_of(f * DEC, DEC), DEC), :],
            (to, t),
        )

    def send_dec_out(k, carry):
        dec_out_piece(k).start()
        return carry

    lax.fori_loop(1, NF, send_dec_out, 0)
    send(T_X2, part.at[4, t_bottom], tx.at[t_bottom], xt)
    own_rows = pl.ds(pl.multiple_of(f * DEC, DEC), DEC)
    own_part = local(dp.at[own_rows, :], dpr.at[own_rows, :], L_OWN2)
    own_part.start()
    def input_half(rows, i):
        total = part[0, rows].astype(F32) + tm[0, rows].astype(F32) + tp[0, rows].astype(F32) + tx[rows, :].astype(F32)
        ig[rows, :] = total.astype(BF)
        store = local(ig.at[rows], ig_o.at[rows], i)
        store.start()
        stores.append(store)

    ring_arrived(0)
    arrived(T_X, tx.at[t_top], xt)
    input_half(t_top, L_IG)
    load_lens.wait()
    load_kc.wait()
    load_vc.wait()

    def dec_out_arrived(k, carry):
        at = pl.ds(pl.multiple_of(peer(NF - k) * DEC, DEC), DEC)
        arrived(D_OUT + k, dpr.at[at, :], (peer(k), t))
        return carry

    lax.fori_loop(1, NF, dec_out_arrived, 0)
    own_part.wait()
    dsum = dpr[0:DEC, :].astype(F32)
    for k in range(1, NF):
        dsum = dsum + dpr[k * DEC:(k + 1) * DEC, :].astype(F32)
    dsum = dsum.astype(BF)

    dec_q = dsum[:, :QC].astype(F32)
    dec_k = dsum[:, QC:QC + HD]
    dec_v = dsum[:, QC + HD:]
    n_q = 2 * GROUPS
    place = lax.broadcasted_iota(jnp.int32, (n_q, CACHE), 1)
    queries = []
    for r in range(DROWS):
        q = jnp.concatenate([dec_q[2 * r:2 * r + 2, g * HD:(g + 1) * HD] for g in range(GROUPS)], axis=0)
        queries.append(q)
        older[r * n_q:(r + 1) * n_q, :] = jnp.where(place < lens[r], f32_dot_nt(q.astype(BF), kc[r]) * scale, MASKED)
    n_all = DROWS * n_q
    new_col = lax.broadcasted_iota(jnp.int32, (n_all, DEC), 1)
    new_row = lax.broadcasted_iota(jnp.int32, (n_all, DEC), 0)
    visible = (new_col // 2 == new_row // n_q) & (new_col % 2 <= new_row % 2)
    newer = f32_dot_nt(jnp.concatenate(queries, axis=0).astype(BF), dec_k) * scale
    newer = jnp.where(visible, newer, MASKED)
    best = jnp.maximum(jnp.max(older[...], 1, keepdims=True), jnp.max(newer, 1, keepdims=True))
    exp_old = jnp.exp(older[...] - best)
    exp_new = jnp.exp(newer - best)
    inv = 1.0 / (jnp.sum(exp_old, 1, keepdims=True) + jnp.sum(exp_new, 1, keepdims=True))
    older[...] = exp_old * inv
    from_new = f32_dot((exp_new * inv).astype(BF), dec_v)
    for r in range(DROWS):
        at = slice(r * n_q, (r + 1) * n_q)
        mixed = f32_dot(older[at, :].astype(BF), vc[r]) + from_new[at, :]
        for g in range(GROUPS):
            dout[2 * r:2 * r + 2, g * HD:(g + 1) * HD] = mixed[2 * g:2 * g + 2, :]

    store_do = local(dout, do_o, L_DO)
    store_do.start()
    stores.append(store_do)

    arrived(T_X2, tx.at[t_bottom], xt)
    input_half(t_bottom, L_IG2)
    for m in sent:
        m.wait_send()

    def sent_small(k, carry):
        dec_piece(k).wait_send()
        dec_out_piece(k).wait_send()
        return carry

    lax.fori_loop(1, NF, sent_small, 0)

    def sent_sib(i, carry):
        to_sib(i).wait_send()
        return carry

    lax.fori_loop(0, 8, sent_sib, 0)
    for m in stores:
        m.wait()


def hand_out(*refs):
    given, out, held, cast, sem = refs[:5], refs[5:10], refs[10:15], refs[15], refs[16]
    sources = (*held[:4], cast)
    into = [pltpu.make_async_copy(given[i], held[i], sem.at[i]) for i in range(5)]
    back = [pltpu.make_async_copy(sources[i], out[i], sem.at[5 + i]) for i in range(5)]
    for m in into:
        m.start()
    for i in range(5):
        into[i].wait()
        if i == 4:
            for r in range(DROWS):
                cast[r] = held[4][2 * r:2 * r + 2, :].astype(BF)
        back[i].start()
    for n in back:
        n.wait()


def on_device(tokens, token_ids, out_grad, w_query, w_key, w_value, dec_states, cache_lens, key_cache, value_cache):
    anywhere = pl.BlockSpec(memory_space=pl.ANY)

    def buf(*shape, dtype=BF):
        return pltpu.VMEM(shape, dtype)

    shapes = [(ROWS, QC), (ROWS, HD), (ROWS, HD), (TOK, FEAT), (DEC, QC)]
    results = pl.pallas_call(
        kernel,
        out_shape=[jax.ShapeDtypeStruct(s, F32 if s[0] == DEC else BF) for s in shapes],
        in_specs=[anywhere] * 10,
        out_specs=[anywhere] * 5,
        scratch_shapes=[
            buf(TOK, D), buf(D, TOK), buf(NF, ROWS, COLS), buf(TOK, COLS, dtype=F32), buf(TOK, COLS), buf(TOK, QC),
            buf(TOK, TOK, dtype=F32), buf(TOK, COLS), buf(HD, TOK), buf(TOK, HD, dtype=F32), buf(TOK, HD, dtype=F32),
            buf(8, ROWS, COLS), buf(8, ROWS, COLS),
            buf(ROWS, COLS), buf(ROWS, COLS), buf(ROWS, COLS), buf(ROWS, COLS), buf(ROWS, COLS), buf(ROWS, COLS),
            buf(HALF, COLS), buf(HALF, COLS),
            buf(8, TOK, FEAT), buf(2, TOK // 2, FEAT), buf(2, TOK // 2, FEAT), buf(2, TOK, FEAT), buf(2, TOK, FEAT),
            buf(TOK, FEAT), buf(TOK, FEAT), buf(ROWS, COLS),
            buf(1, TOK, dtype=jnp.int32), pltpu.SMEM((DROWS,), jnp.int32),
            buf(DROWS, CACHE, HD), buf(DROWS, CACHE, HD),
            buf(DROWS, 2, D), buf(DEC, D, dtype=F32), buf(DEC, D), buf(NF * DEC, ROWS), buf(NF * DEC, COLS), buf(NF * DEC, COLS), buf(DEC, QC, dtype=F32),
            buf(DROWS * 2 * GROUPS, CACHE, dtype=F32),
            pltpu.SemaphoreType.DMA((N_MSG,)), pltpu.SemaphoreType.DMA((N_MSG,)), pltpu.SemaphoreType.DMA((N_LOCAL,)),
        ],
        compiler_params=pltpu.CompilerParams(collective_id=0, has_side_effects=True, vmem_limit_bytes=60 << 20),
        cost_estimate=pl.CostEstimate(flops=13 * 10**9, bytes_accessed=16 * 10**6, transcendentals=2 * 10**6),
    )(
        token_ids.reshape(1, TOK), cache_lens, tokens, out_grad, w_query, w_key, w_value,
        dec_states, key_cache, value_cache,
    )
    shapes[4] = (DROWS, 2, QC)
    return tuple(
        pl.pallas_call(
            hand_out,
            out_shape=[jax.ShapeDtypeStruct(s, BF) for s in shapes],
            in_specs=[anywhere] * 5,
            out_specs=[anywhere] * 5,
            scratch_shapes=[
                *[buf(*s) for s in shapes[:4]], buf(DEC, QC, dtype=F32), buf(*shapes[4]), pltpu.SemaphoreType.DMA((10,)),
            ],
        )(*results)
    )


def solution(mesh):
    placed = (
        P("fsdp", None),
        P("fsdp"),
        P("fsdp", "tensor"),
        P("fsdp", "tensor"),
        P("fsdp", "tensor"),
        P("fsdp", "tensor"),
        P("fsdp", None, None),
        P("fsdp"),
        P("fsdp", None, "tensor"),
        P("fsdp", None, "tensor"),
    )
    return jax.shard_map(
        on_device,
        mesh=mesh,
        in_specs=placed,
        out_specs=(
            P("fsdp", "tensor"),
            P("fsdp", "tensor"),
            P("fsdp", "tensor"),
            P("fsdp", "tensor"),
            P("fsdp", None, "tensor"),
        ),
        check_vma=False,
    )
```

```python
import math

import jax
import jax.numpy as jnp
from jax import lax
from jax.experimental import pallas as pl
from jax.experimental.pallas import tpu as pltpu
from jax.sharding import PartitionSpec as P

MESH = pl.DeviceIdType.MESH
BF = jnp.bfloat16
F32 = jnp.float32

HD = 128
LEARN_RATE = 0.004
BOS_ID = 128000
MASKED = -1e30

TOK = 512
D = 4096
QC = 512
COLS = 768
ROWS = 256
HALF = ROWS // 2
GROUPS = QC // HD
NF = 16
FEAT = 512
DEC = 16
CACHE = 2048
DROWS = 8

G_SIB = 0
G_PT, G_PB, G_MT, G_MB, G_X, G_PF, G_MF, G_XA, G_XB, G_P1, G_M1, G_P2, G_M2 = range(8, 21)
R_SIB = 21
R_X1T, R_X1B, R_PQ, R_MQ, R_PB, R_MB, R_PF, R_MF, R_PA, R_MA, R_X2 = range(29, 40)
T_BASE = 40
T_PF, T_MF, T_PB, T_MB, T_PA, T_MA = range(6)
T_X = 52
D_IN = 53
D_OUT = 69
T_X2 = 85
T_X3 = 86
N_MSG = 87

L_TOK, L_OG, L_WQ, L_WK, L_WV, L_DEC, L_KC, L_VC, L_OWN, L_GQ, L_GK, L_GV, L_IG, L_DO, L_OWN2, L_IDS, L_LENS, L_IG2, L_IG3 = range(19)
N_LOCAL = 19

NT = (((1,), (1,)), ((), ()))


def f32_dot(a, b):
    return jnp.dot(a, b, preferred_element_type=F32)


def f32_dot_nt(a, b):
    return lax.dot_general(a, b, NT, preferred_element_type=F32)


def kernel(
    ids_h, lens_h, tok_h, og_h, wq_h, wk_h, wv_h, dec_h, kc_h, vc_h,
    gq_o, gk_o, gv_o, ig_o, do_o,
    tok, tok_t, w, proj, pb, og, bias, acts, key_t, gk_acc, gv_acc,
    sbs, acc, rx1, rx0, rm, rp, qm, qp, rfm, rfp,
    part, tfm, tfp, tm, tp, tx, ig, gout,
    ids, lens, kc, vc, dec3, dec_f32, dec, dec_in, dp, dpr, dout, older,
    ssem, rsem, lsem,
):
    f = lax.axis_index("fsdp")
    t = lax.axis_index("tensor")
    xh, z, c = f // 8, (f // 2) % 4, f % 2
    xl, y = t // 4, t % 4

    sense = 1 + 2 * c

    def fid(dx, dz, dc):
        return ((xh + dx) % 2) * 8 + ((z + sense * dz) % 4) * 2 + (c + dc) % 2

    def place_of(dx, dz):
        return dx * 4 + (sense * dz) % 4

    def tid(dx, dy):
        return ((xl + dx) % 2) * 4 + (y + dy) % 4

    sib = (fid(0, 0, 1), t)
    zp, zm, xp = (fid(0, 1, 0), t), (fid(0, 3, 0), t), (fid(1, 0, 0), t)
    yp, ym, xt = (f, tid(0, 1)), (f, tid(0, 3)), (f, tid(1, 0))

    def local(src, dst, i):
        return pltpu.make_async_copy(src, dst, lsem.at[i])

    sent = []

    def msg(i, src, dst, to):
        return pltpu.make_async_remote_copy(
            src_ref=src, dst_ref=dst, send_sem=ssem.at[i], recv_sem=rsem.at[i], device_id=to, device_id_type=MESH
        )

    def send(i, src, dst, to):
        m = msg(i, src, dst, to)
        m.start()
        sent.append(m)

    def arrived(i, ref, to):
        msg(i, ref, ref, to).wait_recv()

    def peer(k):
        return lax.rem(f + k, NF)

    near = (sib, zp, zm, xp, yp, ym, xt)
    barrier = pltpu.get_barrier_semaphore()
    for to in near:
        pl.semaphore_signal(barrier, inc=1, device_id=to, device_id_type=MESH)
    own_w = w.at[f]
    loads = [
        local(wq_h, own_w.at[:, pl.ds(0, QC)], L_WQ),
        local(wk_h, own_w.at[:, pl.ds(QC, HD)], L_WK),
        local(wv_h, own_w.at[:, pl.ds(QC + HD, HD)], L_WV),
    ]
    for m in loads:
        m.start()
    load_ids = local(ids_h, ids, L_IDS)
    load_ids.start()
    load_lens = local(lens_h, lens, L_LENS)
    load_lens.start()
    load_tok = local(tok_h, tok, L_TOK)
    load_tok.start()
    load_dec = local(dec_h, dec3, L_DEC)
    load_dec.start()
    load_og = local(og_h, og, L_OG)
    load_og.start()

    for m in loads:
        m.wait()
    pl.semaphore_wait(barrier, len(near))

    top, bottom = pl.ds(0, HALF), pl.ds(HALF, HALF)
    send(G_PT, own_w.at[top], own_w.at[top], zp)
    send(G_MB, own_w.at[bottom], own_w.at[bottom], zm)
    send(G_X, own_w, own_w, xp)
    send(G_PB, own_w.at[bottom], own_w.at[bottom], zp)
    send(G_MT, own_w.at[top], own_w.at[top], zm)
    send(G_SIB + place_of(0, 0), own_w, own_w, sib)

    load_kc = local(kc_h, kc, L_KC)
    load_vc = local(vc_h, vc, L_VC)
    load_kc.start()
    load_vc.start()

    load_ids.wait()
    bos = (ids[...] == BOS_ID).astype(F32)
    row = lax.broadcasted_iota(jnp.int32, (TOK, TOK), 0)
    col = lax.broadcasted_iota(jnp.int32, (TOK, TOK), 1)
    seg_row = f32_dot(jnp.broadcast_to(bos, (16, TOK)).astype(BF), (row <= col).astype(BF))
    seg_col = f32_dot_nt((col <= row).astype(BF), jnp.broadcast_to(bos, (HD, TOK)).astype(BF))
    seg_col = jnp.concatenate([seg_col] * (TOK // HD), axis=1)
    bias[...] = jnp.where((row <= col) & (seg_col == seg_row[0:1, :]), 0.0, MASKED)

    load_dec.wait()
    for r in range(DROWS):
        dec_f32[2 * r:2 * r + 2, :] = dec3[r].astype(F32)
    dec[...] = dec_f32[...].astype(BF)
    load_tok.wait()

    def turn(i, carry):
        at = pl.ds(pl.multiple_of(i * ROWS, ROWS), ROWS)
        tok_t[at, :] = tok[:, at].T
        return carry

    def project(dx, dz, first=False):
        chip = fid(dx, dz, 0) // 2
        at = pl.ds(pl.multiple_of(chip * 2 * ROWS, 2 * ROWS), 2 * ROWS)
        rows = w[pl.ds(chip * 2, 2)].reshape(2 * ROWS, COLS)
        term = f32_dot(tok[:, at], rows)
        proj[...] = term if first else proj[...] + term

    def shard(dx, dz, dc=0):
        return w.at[fid(dx, dz, dc)]

    def pass_on(dx, dz):
        send(G_SIB + place_of(dx, dz), shard(dx, dz), shard(dx, dz), sib)

    def from_sib(dx, dz):
        arrived(G_SIB + place_of(dx, dz), shard(dx, dz, 1), sib)

    def relay(i, ref, to):
        send(i, ref, ref, to)

    from_sib(0, 0)
    project(0, 0, True)
    lax.fori_loop(0, 4, turn, 0)

    arrived(G_PT, shard(0, 3).at[top], zp)
    relay(G_PF, shard(0, 3).at[top], zp)
    relay(G_XA, shard(0, 3).at[top], xp)
    arrived(G_MB, shard(0, 1).at[bottom], zm)
    relay(G_MF, shard(0, 1).at[bottom], zm)
    relay(G_XB, shard(0, 1).at[bottom], xp)
    lax.fori_loop(4, 6, turn, 0)
    arrived(G_X, shard(1, 0), xp)
    relay(G_P1, shard(1, 0).at[bottom], zp)
    relay(G_M1, shard(1, 0).at[top], zm)
    pass_on(1, 0)
    arrived(G_PB, shard(0, 3).at[bottom], zp)
    pass_on(0, 3)
    arrived(G_MT, shard(0, 1).at[top], zm)
    pass_on(0, 1)
    lax.fori_loop(6, 9, turn, 0)
    from_sib(1, 0)
    project(1, 0)
    arrived(G_PF, shard(0, 2).at[top], zp)
    arrived(G_MF, shard(0, 2).at[bottom], zm)
    pass_on(0, 2)
    arrived(G_XA, shard(1, 3).at[top], xp)
    relay(G_P2, shard(1, 3).at[top], zp)
    from_sib(0, 3)
    project(0, 3)
    from_sib(0, 1)
    project(0, 1)
    lax.fori_loop(9, 11, turn, 0)
    arrived(G_XB, shard(1, 1).at[bottom], xp)
    relay(G_M2, shard(1, 1).at[bottom], zm)
    arrived(G_P1, shard(1, 3).at[bottom], zp)
    pass_on(1, 3)
    arrived(G_M1, shard(1, 1).at[top], zm)
    pass_on(1, 1)
    from_sib(0, 2)
    project(0, 2)
    lax.fori_loop(11, NF, turn, 0)
    from_sib(1, 3)
    project(1, 3)
    from_sib(1, 1)
    project(1, 1)
    arrived(G_P2, shard(1, 2).at[top], zp)
    arrived(G_M2, shard(1, 2).at[bottom], zm)
    pass_on(1, 2)
    from_sib(1, 2)
    project(1, 2)

    def dec_piece(k):
        to = peer(k)
        return msg(
            D_IN + k,
            dec.at[:, pl.ds(pl.multiple_of(to * ROWS, ROWS), ROWS)],
            dec_in.at[pl.ds(pl.multiple_of(f * DEC, DEC), DEC), :],
            (to, t),
        )

    def send_dec(k, carry):
        dec_piece(k).start()
        return carry

    lax.fori_loop(1, NF, send_dec, 0)
    own_dec = local(
        dec.at[:, pl.ds(pl.multiple_of(f * ROWS, ROWS), ROWS)],
        dec_in.at[pl.ds(pl.multiple_of(f * DEC, DEC), DEC), :],
        L_OWN,
    )
    own_dec.start()

    pb[...] = proj[...].astype(BF)
    load_og.wait()
    key_t[...] = pb[:, QC:QC + HD].T
    gk_acc[...] = jnp.zeros_like(gk_acc)
    gv_acc[...] = jnp.zeros_like(gv_acc)
    scale = 1.0 / math.sqrt(HD)
    width = TOK // 2

    def head(h, carry):
        at = pl.ds(pl.multiple_of(h * HD, HD), HD)
        for block in range(2):
            qs = pl.ds(block * width, width)
            seen = (block + 1) * width
            ks = pl.ds(0, seen)
            keys = pb[ks, pl.ds(QC, HD)]
            values = pb[ks, pl.ds(QC + HD, HD)]
            query = pb[qs, at]
            upstream = og[qs, at]
            scores = f32_dot_nt(keys, query) * scale + bias[ks, qs]
            expo = jnp.exp(scores - jnp.max(scores, 0, keepdims=True))
            probs = expo * (1.0 / jnp.sum(expo, 0, keepdims=True))
            dprob = f32_dot_nt(values, upstream)
            delta = jnp.sum(probs * dprob, 0, keepdims=True)
            dscore = (probs * (dprob - delta) * scale).astype(BF)
            gv_acc[ks, :] += f32_dot(probs.astype(BF), upstream)
            gk_acc[ks, :] += f32_dot(dscore, query)
            acts[qs, at] = f32_dot(key_t[:, ks], dscore).T.astype(BF)
        return carry

    lax.fori_loop(0, GROUPS, head, 0, unroll=True)
    acts[:, QC:QC + HD] = gk_acc[...].astype(BF)
    acts[:, QC + HD:] = gv_acc[...].astype(BF)

    def grad_block(slot):
        rows = tok_t[pl.ds(pl.multiple_of(slot * ROWS, ROWS), ROWS), :]
        return f32_dot(rows, acts[...])

    def block_of(i, dc):
        return ((xh + i // 4) % 2) * 8 + ((z + i % 4) % 4) * 2 + (c + dc) % 2

    def to_sib(i):
        return msg(R_SIB + i, sbs.at[i], acc.at[i], sib)

    def sib_block(i):
        sbs[i] = grad_block(block_of(i, 1)).astype(BF)
        to_sib(i).start()

    def own_block(i):
        block = grad_block(block_of(i, 0))
        arrived(R_SIB + i, acc.at[i], sib)
        acc[i] = (block + acc[i].astype(F32)).astype(BF)

    def sums(dx, dz, part=None):
        ref = acc.at[place_of(dx, dz)]
        return ref if part is None else ref.at[part]

    def add(dst, *terms):
        total = dst[...].astype(F32)
        for x in terms:
            total = total + x[...].astype(F32)
        dst[...] = total.astype(BF)

    t_top, t_bottom = pl.ds(0, TOK // 2), pl.ds(TOK // 2, TOK // 2)
    t_third, t_last = pl.ds(TOK // 2, TOK // 4), pl.ds(3 * TOK // 4, TOK // 4)

    def input_block(i):
        rows = w[pl.ds(tid(i // 4, i % 4) * 2, 2)].reshape(2 * ROWS, COLS)
        part[i] = f32_dot_nt(acts[...], rows).astype(BF)

    def send_far(dx):
        base, i = T_BASE + dx * 6, dx * 4
        send(base + T_PF, part.at[i + 2, t_top], tfp.at[dx], yp)
        send(base + T_MF, part.at[i + 2, t_bottom], tfm.at[dx], ym)

    def send_near(dx):
        base, i = T_BASE + dx * 6, dx * 4
        send(base + T_PB, part.at[i + 1, t_bottom], tm.at[dx, t_bottom], yp)
        send(base + T_MB, part.at[i + 3, t_top], tp.at[dx, t_top], ym)

    def send_relayed(dx):
        base, i = T_BASE + dx * 6, dx * 4
        arrived(base + T_PF, tfp.at[dx], yp)
        add(part.at[i + 1, t_top], tfp.at[dx])
        send(base + T_PA, part.at[i + 1, t_top], tm.at[dx, t_top], yp)
        arrived(base + T_MF, tfm.at[dx], ym)
        add(part.at[i + 3, t_bottom], tfm.at[dx])
        send(base + T_MA, part.at[i + 3, t_bottom], tp.at[dx, t_bottom], ym)

    def ring_arrived(dx):
        base = T_BASE + dx * 6
        arrived(base + T_PB, tm.at[dx, t_bottom], yp)
        arrived(base + T_MB, tp.at[dx, t_top], ym)
        arrived(base + T_PA, tm.at[dx, t_top], yp)
        arrived(base + T_MA, tp.at[dx, t_bottom], ym)

    input_block(6)
    send_far(1)
    for i in (6, 5, 7):
        sib_block(i)
    own_block(6)
    send(R_X1T, sums(1, 2, top), rx1.at[top], xp)
    send(R_X1B, sums(1, 2, bottom), rx1.at[bottom], xp)
    own_block(5)
    own_block(7)
    send(R_PQ, sums(1, 1), qm, zp)
    send(R_MQ, sums(1, 3), qp, zm)
    input_block(5)
    input_block(7)
    send_near(1)
    for i in (2, 1, 3, 4, 0):
        sib_block(i)
    input_block(2)
    input_block(1)
    input_block(3)

    send_relayed(1)
    send_far(0)
    send_near(0)
    for i in (2, 1, 3, 4, 0):
        own_block(i)
    arrived(R_X1T, rx1.at[top], xp)
    add(sums(0, 2, top), rx1.at[top])
    send(R_PF, sums(0, 2, top), rfp, zp)
    send(R_PB, sums(0, 1, bottom), rm.at[bottom], zp)
    send(R_MB, sums(0, 3, top), rp.at[top], zm)
    arrived(R_X1B, rx1.at[bottom], xp)
    add(sums(0, 2, bottom), rx1.at[bottom])
    send(R_MF, sums(0, 2, bottom), rfm, zm)
    input_block(4)
    arrived(R_PQ, qm, zp)
    arrived(R_MQ, qp, zm)
    add(sums(1, 0), qm, qp)
    send(R_X2, sums(1, 0), rx0, xp)
    input_block(0)
    arrived(R_PF, rfp, zp)
    add(sums(0, 1, top), rfp)
    send(R_PA, sums(0, 1, top), rm.at[top], zp)
    ring_arrived(1)
    add(part.at[4], tm.at[1], tp.at[1])
    send(T_X, part.at[4, t_top], tx.at[t_top], xt)
    arrived(R_MF, rfm, zm)
    add(sums(0, 3, bottom), rfm)
    send(R_MA, sums(0, 3, bottom), rp.at[bottom], zm)
    send_relayed(0)

    arrived(R_PB, rm.at[bottom], zp)
    arrived(R_MB, rp.at[top], zm)
    arrived(R_PA, rm.at[top], zp)
    arrived(R_MA, rp.at[bottom], zm)
    arrived(R_X2, rx0, xp)
    total = sums(0, 0)[...].astype(F32) + rm[...].astype(F32) + rp[...].astype(F32) + rx0[...].astype(F32)
    grad = (total * (1.0 / NF)).astype(BF)
    gout[...] = grad
    stores = [
        local(gout.at[:, pl.ds(0, QC)], gq_o, L_GQ),
        local(gout.at[:, pl.ds(QC, HD)], gk_o, L_GK),
        local(gout.at[:, pl.ds(QC + HD, HD)], gv_o, L_GV),
    ]
    for m in stores:
        m.start()
    fresh = (own_w[...].astype(F32) - LEARN_RATE * grad.astype(F32)).astype(BF)

    def dec_arrived(k, carry):
        at = pl.ds(pl.multiple_of(peer(NF - k) * DEC, DEC), DEC)
        arrived(D_IN + k, dec_in.at[at, :], (peer(k), t))
        return carry

    lax.fori_loop(1, NF, dec_arrived, 0)
    own_dec.wait()
    dp[...] = f32_dot(dec_in[...], fresh).astype(BF)

    def dec_out_piece(k):
        to = peer(k)
        return msg(
            D_OUT + k,
            dp.at[pl.ds(pl.multiple_of(to * DEC, DEC), DEC), :],
            dpr.at[pl.ds(pl.multiple_of(f * DEC, DEC), DEC), :],
            (to, t),
        )

    def send_dec_out(k, carry):
        dec_out_piece(k).start()
        return carry

    lax.fori_loop(1, NF, send_dec_out, 0)
    send(T_X2, part.at[4, t_third], tx.at[t_third], xt)
    send(T_X3, part.at[4, t_last], tx.at[t_last], xt)
    own_rows = pl.ds(pl.multiple_of(f * DEC, DEC), DEC)
    own_part = local(dp.at[own_rows, :], dpr.at[own_rows, :], L_OWN2)
    own_part.start()
    def input_half(rows, i):
        total = part[0, rows].astype(F32) + tm[0, rows].astype(F32) + tp[0, rows].astype(F32) + tx[rows, :].astype(F32)
        ig[rows, :] = total.astype(BF)
        store = local(ig.at[rows], ig_o.at[rows], i)
        store.start()
        stores.append(store)

    ring_arrived(0)
    arrived(T_X, tx.at[t_top], xt)
    input_half(t_top, L_IG)
    load_lens.wait()
    load_kc.wait()
    load_vc.wait()

    def dec_out_arrived(k, carry):
        at = pl.ds(pl.multiple_of(peer(NF - k) * DEC, DEC), DEC)
        arrived(D_OUT + k, dpr.at[at, :], (peer(k), t))
        return carry

    lax.fori_loop(1, NF, dec_out_arrived, 0)
    own_part.wait()
    dsum = dpr[0:DEC, :].astype(F32)
    for k in range(1, NF):
        dsum = dsum + dpr[k * DEC:(k + 1) * DEC, :].astype(F32)
    dsum = dsum.astype(BF)

    dec_q = dsum[:, :QC].astype(F32)
    dec_k = dsum[:, QC:QC + HD]
    dec_v = dsum[:, QC + HD:]
    n_q = 2 * GROUPS
    place = lax.broadcasted_iota(jnp.int32, (n_q, CACHE), 1)
    queries = []
    for r in range(DROWS):
        q = jnp.concatenate([dec_q[2 * r:2 * r + 2, g * HD:(g + 1) * HD] for g in range(GROUPS)], axis=0)
        queries.append(q)
        older[r * n_q:(r + 1) * n_q, :] = jnp.where(place < lens[r], f32_dot_nt(q.astype(BF), kc[r]) * scale, MASKED)
    n_all = DROWS * n_q
    new_col = lax.broadcasted_iota(jnp.int32, (n_all, DEC), 1)
    new_row = lax.broadcasted_iota(jnp.int32, (n_all, DEC), 0)
    visible = (new_col // 2 == new_row // n_q) & (new_col % 2 <= new_row % 2)
    newer = f32_dot_nt(jnp.concatenate(queries, axis=0).astype(BF), dec_k) * scale
    newer = jnp.where(visible, newer, MASKED)
    best = jnp.maximum(jnp.max(older[...], 1, keepdims=True), jnp.max(newer, 1, keepdims=True))
    exp_old = jnp.exp(older[...] - best)
    exp_new = jnp.exp(newer - best)
    inv = 1.0 / (jnp.sum(exp_old, 1, keepdims=True) + jnp.sum(exp_new, 1, keepdims=True))
    older[...] = exp_old * inv
    from_new = f32_dot((exp_new * inv).astype(BF), dec_v)
    for r in range(DROWS):
        at = slice(r * n_q, (r + 1) * n_q)
        mixed = f32_dot(older[at, :].astype(BF), vc[r]) + from_new[at, :]
        for g in range(GROUPS):
            dout[2 * r:2 * r + 2, g * HD:(g + 1) * HD] = mixed[2 * g:2 * g + 2, :]

    store_do = local(dout, do_o, L_DO)
    store_do.start()
    stores.append(store_do)

    arrived(T_X2, tx.at[t_third], xt)
    input_half(t_third, L_IG2)
    arrived(T_X3, tx.at[t_last], xt)
    input_half(t_last, L_IG3)
    for m in sent:
        m.wait_send()

    def sent_small(k, carry):
        dec_piece(k).wait_send()
        dec_out_piece(k).wait_send()
        return carry

    lax.fori_loop(1, NF, sent_small, 0)

    def sent_sib(i, carry):
        to_sib(i).wait_send()
        return carry

    lax.fori_loop(0, 8, sent_sib, 0)
    for m in stores:
        m.wait()


def hand_out(*refs):
    given, out, held, cast, sem = refs[:5], refs[5:10], refs[10:15], refs[15], refs[16]
    sources = (*held[:4], cast)
    into = [pltpu.make_async_copy(given[i], held[i], sem.at[i]) for i in range(5)]
    back = [pltpu.make_async_copy(sources[i], out[i], sem.at[5 + i]) for i in range(5)]
    for m in into:
        m.start()
    for i in range(5):
        into[i].wait()
        if i == 4:
            for r in range(DROWS):
                cast[r] = held[4][2 * r:2 * r + 2, :].astype(BF)
        back[i].start()
    for n in back:
        n.wait()


def on_device(tokens, token_ids, out_grad, w_query, w_key, w_value, dec_states, cache_lens, key_cache, value_cache):
    anywhere = pl.BlockSpec(memory_space=pl.ANY)

    def buf(*shape, dtype=BF):
        return pltpu.VMEM(shape, dtype)

    shapes = [(ROWS, QC), (ROWS, HD), (ROWS, HD), (TOK, FEAT), (DEC, QC)]
    results = pl.pallas_call(
        kernel,
        out_shape=[jax.ShapeDtypeStruct(s, F32 if s[0] == DEC else BF) for s in shapes],
        in_specs=[anywhere] * 10,
        out_specs=[anywhere] * 5,
        scratch_shapes=[
            buf(TOK, D), buf(D, TOK), buf(NF, ROWS, COLS), buf(TOK, COLS, dtype=F32), buf(TOK, COLS), buf(TOK, QC),
            buf(TOK, TOK, dtype=F32), buf(TOK, COLS), buf(HD, TOK), buf(TOK, HD, dtype=F32), buf(TOK, HD, dtype=F32),
            buf(8, ROWS, COLS), buf(8, ROWS, COLS),
            buf(ROWS, COLS), buf(ROWS, COLS), buf(ROWS, COLS), buf(ROWS, COLS), buf(ROWS, COLS), buf(ROWS, COLS),
            buf(HALF, COLS), buf(HALF, COLS),
            buf(8, TOK, FEAT), buf(2, TOK // 2, FEAT), buf(2, TOK // 2, FEAT), buf(2, TOK, FEAT), buf(2, TOK, FEAT),
            buf(TOK, FEAT), buf(TOK, FEAT), buf(ROWS, COLS),
            buf(1, TOK, dtype=jnp.int32), pltpu.SMEM((DROWS,), jnp.int32),
            buf(DROWS, CACHE, HD), buf(DROWS, CACHE, HD),
            buf(DROWS, 2, D), buf(DEC, D, dtype=F32), buf(DEC, D), buf(NF * DEC, ROWS), buf(NF * DEC, COLS), buf(NF * DEC, COLS), buf(DEC, QC, dtype=F32),
            buf(DROWS * 2 * GROUPS, CACHE, dtype=F32),
            pltpu.SemaphoreType.DMA((N_MSG,)), pltpu.SemaphoreType.DMA((N_MSG,)), pltpu.SemaphoreType.DMA((N_LOCAL,)),
        ],
        compiler_params=pltpu.CompilerParams(collective_id=0, has_side_effects=True, vmem_limit_bytes=60 << 20),
        cost_estimate=pl.CostEstimate(flops=13 * 10**9, bytes_accessed=16 * 10**6, transcendentals=2 * 10**6),
    )(
        token_ids.reshape(1, TOK), cache_lens, tokens, out_grad, w_query, w_key, w_value,
        dec_states, key_cache, value_cache,
    )
    shapes[4] = (DROWS, 2, QC)
    return tuple(
        pl.pallas_call(
            hand_out,
            out_shape=[jax.ShapeDtypeStruct(s, BF) for s in shapes],
            in_specs=[anywhere] * 5,
            out_specs=[anywhere] * 5,
            scratch_shapes=[
                *[buf(*s) for s in shapes[:4]], buf(DEC, QC, dtype=F32), buf(*shapes[4]), pltpu.SemaphoreType.DMA((10,)),
            ],
        )(*results)
    )


def solution(mesh):
    placed = (
        P("fsdp", None),
        P("fsdp"),
        P("fsdp", "tensor"),
        P("fsdp", "tensor"),
        P("fsdp", "tensor"),
        P("fsdp", "tensor"),
        P("fsdp", None, None),
        P("fsdp"),
        P("fsdp", None, "tensor"),
        P("fsdp", None, "tensor"),
    )
    return jax.shard_map(
        on_device,
        mesh=mesh,
        in_specs=placed,
        out_specs=(
            P("fsdp", "tensor"),
            P("fsdp", "tensor"),
            P("fsdp", "tensor"),
            P("fsdp", "tensor"),
            P("fsdp", None, "tensor"),
        ),
        check_vma=False,
    )
```
